512 devices in a mesh: dp: 16 (over y, x_hi, core), row: 32 (over x_lo, z).
Axes of the slice: x: 4 (x_hi: 2, x_lo: 2; x = x_hi * 2 + x_lo), y: 4, z: 16, core: 2. Of those that a mesh axis runs over, the one named last changes fastest.
Arguments:
- embedding_row_values: bfloat16 [26, 8192, 128], P(None, 'row'), may hold values from -2 to 2
- accum: float32 [26, 8192], P(None, 'row'), may hold values from 0.01 to 0.1
- bag_ids: int32 [8192, 26, 8], P('dp'), may hold values from 0 to 8191
- cross_v: bfloat16 [3328, 256], P('row'), may hold values from -0.109375 to 0.109375
- cross_u: bfloat16 [3328, 256], P('row'), may hold values from -0.375 to 0.375
- cross_bias: float32 [3328], P('row'), may hold values from -3 to 3
- upstream: bfloat16 [8192, 3328], P('dp', 'row'), may hold values from -0.125 to 0.125
Outputs:
- crossed: bfloat16 [8192, 3328], P('dp', 'row')
- new_rows: bfloat16 [26, 8192, 128], P(None, 'row')
- new_accum: float32 [26, 8192], P(None, 'row')
- grad_v: float32 [3328, 256], P('row')
- grad_u: float32 [3328, 256], P('row')
- grad_bias: float32 [3328], P('row')
The draws below stay inside these ranges and needn't reach their ends.
All inputs are finite; a program needn't handle non-finite values.
Results may differ from the reference program's by a relative error of at most 0.0068.
Values may be sent and summed in bfloat16 or wider, within the bound.
No kernel may reach another device: no remote copies, remote signals or barrier semaphores. Data moves between devices by JAX's collectives and lax.ppermute only.
A program may use at most 64 MiB of HBM per device.

```python
import math
import jax
import jax.numpy as jnp
from jax import lax

NT = 26
ED = 128
RANK = 256
BAG = 8
ROWS_DEV = 256
FEAT = 3328
SAMPLES = 8192
ROWS = 8192
N_ROW = 32


def plant(result, rng, least, top_value):
    spot = [jax.random.randint(jax.random.fold_in(rng, axis), (), 0, length) for axis, length in enumerate(result.shape)]
    main_axis = result.shape.index(max(result.shape))
    beside = spot[:main_axis] + [(spot[main_axis] + 1) % result.shape[main_axis]] + spot[main_axis + 1:]
    return result.at[tuple(spot)].set(least).at[tuple(beside)].set(top_value)


def levels(key, shape, split, low, largest):
    factor_of = 1.0
    for axis_at, shards_of in split:
        heights = jax.random.uniform(jax.random.fold_in(jax.random.fold_in(key, 6), axis_at), (shards_of,), jnp.float32, low / len(split), largest / len(split))
        factor_of = factor_of * jnp.repeat(jnp.exp(heights), shape[axis_at] // shards_of).reshape((-1,) + (1,) * (len(shape) - 1 - axis_at))
    return factor_of


def centred(own_key, dims, scale, reach, cuts=(), kind=jnp.bfloat16):
    entries = jax.random.normal(own_key, dims, jnp.float32) * scale
    if len(cuts) > 0:
        entries = levels(own_key, dims, cuts, -0.22, 0.18) * entries
    return jnp.clip(entries, min=-reach, max=reach).astype(kind)


def setup_inputs(seed: int = 0) -> dict:
    key_of = jax.random.split(jax.random.key(seed), 8)
    return {
        "embedding_row_values": centred(key_of[0], (NT, ROWS, ED), 0.35, 2.0, ((1, 32),)),
        "accum": jnp.clip(jnp.exp(math.log(0.1) - 2.3025851 * jax.random.uniform(key_of[1], (NT, ROWS), jnp.float32) ** levels(key_of[1], (NT, ROWS), ((1, 32),), -0.2, 0.2)), 0.01, 0.1),
        "bag_ids": plant(jax.random.randint(key_of[2], (SAMPLES, NT, BAG), 0, ROWS_DEV * N_ROW), jax.random.fold_in(key_of[2], 1), 0, (ROWS_DEV * N_ROW) - 1).astype(jnp.int32),
        "cross_v": centred(key_of[3], (FEAT, RANK), (NT * ED) ** -0.5, 0.109375, ((0, 32),)),
        "cross_u": centred(key_of[4], (FEAT, RANK), RANK ** -0.5, 0.375, ((0, 32),)),
        "cross_bias": centred(key_of[5], (FEAT,), 0.5, 3.0, ((0, 32),), jnp.float32),
        "upstream": centred(key_of[6], (SAMPLES, FEAT), 0.02, 0.125, ((0, 16), (1, 32))),
    }


learn_rate = 0.3
epsilon = 1e-06

def pool_table(operands):
    table_rows, table_ids = operands
    fetched_embeddings = table_rows[table_ids].astype(jnp.float32)
    owner_row = table_ids // ROWS_DEV
    owning_devices = (owner_row[:, :, None] == jnp.arange(N_ROW, dtype=jnp.int32)[None, None, :]).astype(jnp.float32)
    partial_cross_value = jnp.einsum('dcg,dch->dgh', owning_devices, fetched_embeddings, precision=lax.Precision.HIGHEST)
    partial_cross_value = lax.optimization_barrier(partial_cross_value.astype(jnp.bfloat16)).astype(jnp.float32)
    return lax.optimization_barrier(jnp.sum(partial_cross_value, axis=1)).astype(jnp.bfloat16)

def block_sum(left_side, right_side):
    return jnp.dot(left_side, right_side, preferred_element_type=jnp.float32)

def table_grad(operands):
    table_ids_one, grads_one = operands
    spread = jnp.broadcast_to(grads_one.astype(jnp.float32)[:, None, :], (grads_one.shape[0], BAG, ED)).reshape(-1, ED)
    return jax.ops.segment_sum(spread, table_ids_one.reshape(-1), num_segments=ROWS_DEV * N_ROW)

def reference(embedding_row_values, accum, bag_ids, cross_v, cross_u, cross_bias, upstream):
    table_ids = jnp.transpose(bag_ids, (1, 0, 2))
    pooled = lax.map(pool_table, (embedding_row_values, table_ids))
    pooled = jnp.transpose(pooled, (1, 0, 2)).reshape(bag_ids.shape[0], NT * ED)
    rank_bf = block_sum(pooled, cross_v).astype(jnp.bfloat16)
    gate_term = jnp.dot(rank_bf, cross_u.T, preferred_element_type=jnp.float32) + cross_bias
    pooled_f = pooled.astype(jnp.float32)
    crossed = (pooled_f * gate_term + pooled_f).astype(jnp.bfloat16)
    cotangent = upstream.astype(jnp.float32)
    gate_grad = cotangent * pooled_f
    gate_bf = gate_grad.astype(jnp.bfloat16)
    grad_u = jnp.dot(gate_bf.T, rank_bf, preferred_element_type=jnp.float32)
    grad_bias = lax.optimization_barrier(jnp.sum(gate_grad, axis=0))
    rank_grad = block_sum(gate_bf, cross_u).astype(jnp.bfloat16)
    grad_v = jnp.dot(pooled.T, rank_grad, preferred_element_type=jnp.float32)
    back_proj = jnp.dot(rank_grad, cross_v.T, preferred_element_type=jnp.float32)
    pooled_grad = (cotangent * (gate_term + 1.0) + back_proj).astype(jnp.bfloat16)
    grad_tables = jnp.transpose(pooled_grad.reshape(pooled_grad.shape[0], NT, ED), (1, 0, 2))
    row_grad = lax.map(table_grad, (table_ids, grad_tables))
    new_accum = accum + lax.optimization_barrier(jnp.mean(row_grad * row_grad, axis=2))
    step_scale = lax.rsqrt(new_accum + epsilon)
    new_rows = (embedding_row_values.astype(jnp.float32) - learn_rate * row_grad * step_scale[:, :, None]).astype(jnp.bfloat16)
    return (crossed, new_rows, new_accum, grad_v, grad_u, grad_bias)
```

```python
import jax
import jax.numpy as jnp
from jax import lax
from jax.experimental import pallas as pl
from jax.experimental.pallas import tpu as pltpu
from jax.sharding import Mesh
from jax.sharding import PartitionSpec as P

bf16 = jnp.bfloat16
f32 = jnp.float32
learn_rate = 0.3
epsilon = 1e-06

SAMPLES, TABLES, BAG, ROWS, WIDTH, FEATS, RANK = 512, 26, 8, 256, 128, 104, 256
N_ROW, N_DP, PART = 32, 16, 16
STEP_ROWS = N_ROW * PART
WORDS = STEP_ROWS // 8
GRAD_ROWS = 8
OUT_ROWS = FEATS + GRAD_ROWS
DP_OUTER = ("y", "x_hi")
VMEM = 40 << 20

NT_DIMS = (((1,), (1,)), ((), ()))
TN_DIMS = (((0,), (0,)), ((), ()))


def counts_of(words):
    columns = []
    for lane in range(0, SAMPLES, 128):
        blocks = []
        for group in range(0, WORDS, 8):
            word = words[group : group + 8, lane : lane + 128]
            digits = [lax.shift_right_logical(word, jnp.int32(4 * j)) & 15 for j in range(8)]
            blocks.append(jnp.concatenate(digits, axis=0).astype(f32).astype(bf16))
        columns.append(jnp.concatenate(blocks, axis=0))
    return jnp.concatenate(columns, axis=1)


def words_of(place):
    inside = (place >= 0) & (place < STEP_ROWS)
    word = jnp.where(inside, ((place >> 6) << 3) | (place & 7), -1)
    unit = jnp.left_shift(jnp.int32(1), ((place >> 3) & 7) * 4)
    columns = []
    for lane in range(0, SAMPLES, 128):
        slots = lax.broadcasted_iota(jnp.int32, (WORDS, 128), 0)
        total = jnp.zeros((WORDS, 128), jnp.int32)
        for k in range(BAG):
            here = word[k : k + 1, lane : lane + 128] == slots
            total = total + jnp.where(here, unit[k : k + 1, lane : lane + 128], 0)
        columns.append(total)
    return jnp.concatenate(columns, axis=1)


def forward_kernel(
    scalars, ids_a, ids_b, own, other, v, u, upstream, pooled_out, words_out, ranks_out, places, total
):
    step = pl.program_id(0)
    core = scalars[2]

    @pl.when(step == 0)
    def _():
        total[...] = jnp.zeros_like(total)
        for table, ids in enumerate((ids_a, ids_b)):
            row = ids[0]
            part = (row >> 4) & 15
            turn = (part & 1) ^ core
            places[table] = turn * 4096 + (part >> 1) * 512 + (row >> 8) * 16 + (row & 15)

    rows = jnp.where(step < 8, own[0].astype(f32), other[0].astype(f32)).astype(bf16)
    for table in range(2):
        words = words_of(places[table] - step * STEP_ROWS)
        words_out[table, 0] = words
        total[table] += jnp.dot(rows, counts_of(words), preferred_element_type=f32)

    @pl.when(step == N_DP - 1)
    def _():
        feature = lax.broadcasted_iota(jnp.int32, (FEATS, SAMPLES), 0)
        pooled = jnp.where(feature < scalars[3], total[0], total[1]).astype(bf16)
        pooled_out[...] = pooled
        gate_grad = (upstream[...].astype(f32) * pooled.astype(f32)).astype(bf16)
        ranks_out[:RANK] = lax.dot_general(v[...], pooled, TN_DIMS, preferred_element_type=f32).astype(bf16)
        ranks_out[RANK:] = lax.dot_general(u[...], gate_grad, TN_DIMS, preferred_element_type=f32).astype(bf16)


def forward(scalars, ids, own, other, v, u, upstream):
    whole = lambda *shape: pl.BlockSpec(shape, lambda g, s: (0,) * len(shape))
    return pl.pallas_call(
        forward_kernel,
        grid_spec=pltpu.PrefetchScalarGridSpec(
            num_scalar_prefetch=1,
            grid=(N_DP,),
            in_specs=[
                pl.BlockSpec((1, BAG, SAMPLES), lambda g, s: (s[0], 0, 0)),
                pl.BlockSpec((1, BAG, SAMPLES), lambda g, s: (s[1], 0, 0)),
                pl.BlockSpec((1, FEATS, STEP_ROWS), lambda g, s: (jnp.minimum(g, 7), 0, 0)),
                pl.BlockSpec((1, FEATS, STEP_ROWS), lambda g, s: (jnp.maximum(g - 8, 0), 0, 0)),
                whole(FEATS, RANK),
                whole(FEATS, RANK),
                whole(FEATS, SAMPLES),
            ],
            out_specs=[
                whole(FEATS, SAMPLES),
                pl.BlockSpec((2, 1, WORDS, SAMPLES), lambda g, s: (0, g, 0, 0)),
                whole(2 * RANK, SAMPLES),
            ],
            scratch_shapes=[
                pltpu.VMEM((2, BAG, SAMPLES), jnp.int32),
                pltpu.VMEM((2, FEATS, SAMPLES), f32),
            ],
        ),
        out_shape=[
            jax.ShapeDtypeStruct((FEATS, SAMPLES), bf16),
            jax.ShapeDtypeStruct((2, N_DP, WORDS, SAMPLES), jnp.int32),
            jax.ShapeDtypeStruct((2 * RANK, SAMPLES), bf16),
        ],
        compiler_params=pltpu.CompilerParams(vmem_limit_bytes=VMEM),
        name="bags_and_ranks",
    )(scalars, ids, ids, own, other, v, u, upstream)


def backward_kernel(
    scalars, words, ranks, pooled_in, v, u, bias, upstream_in, crossed_out, own_out, other_out, grads, cross_grads
):
    step = pl.program_id(0)

    @pl.when(step == 0)
    def _():
        rank = ranks[:RANK]
        rank_grad = ranks[RANK:]
        pooled_bf = pooled_in[...]
        pooled = pooled_bf.astype(f32)
        upstream = upstream_in[...].astype(f32)
        gate = jnp.dot(u[...], rank, preferred_element_type=f32) + bias[...]
        crossed_out[...] = (pooled * gate + pooled).astype(bf16)
        back = jnp.dot(v[...], rank_grad, preferred_element_type=f32)
        grad = (upstream * (gate + 1.0) + back).astype(bf16).astype(f32)
        feature = lax.broadcasted_iota(jnp.int32, (FEATS, SAMPLES), 0)
        grads[0] = jnp.where(feature < scalars[1], grad, 0.0).astype(bf16)
        grads[1] = jnp.where(feature < scalars[1], 0.0, grad).astype(bf16)
        gate_grad = upstream * pooled
        gate_bf = gate_grad.astype(bf16)
        gate_rest = (gate_grad - gate_bf.astype(f32)).astype(bf16)
        cross_grads[...] = jnp.zeros_like(cross_grads)
        cross_grads[:FEATS, :RANK] = lax.dot_general(gate_bf, rank, NT_DIMS, preferred_element_type=f32)
        cross_grads[:FEATS, RANK:] = lax.dot_general(pooled_bf, rank_grad, NT_DIMS, preferred_element_type=f32)
        ones = jnp.ones((16, SAMPLES), bf16)
        bias_sum = lax.dot_general(ones, gate_bf, NT_DIMS, preferred_element_type=f32) + lax.dot_general(
            ones, gate_rest, NT_DIMS, preferred_element_type=f32
        )
        cross_grads[FEATS : FEATS + 8, :FEATS] = bias_sum[:8]

    turn = step // 8
    part = 2 * (step - 8 * turn) + (turn ^ scalars[0])
    result = lax.dot_general(grads[0], counts_of(words[0, 0]), NT_DIMS, preferred_element_type=f32)
    result = result + lax.dot_general(grads[1], counts_of(words[1, 0]), NT_DIMS, preferred_element_type=f32)
    extra = cross_grads[pl.ds(pl.multiple_of(part * GRAD_ROWS, GRAD_ROWS), GRAD_ROWS), :]
    block = jnp.concatenate([result, extra], axis=0).astype(bf16)

    @pl.when(turn == 0)
    def _():
        own_out[0] = block

    @pl.when(turn == 1)
    def _():
        other_out[0] = block


def backward(scalars, words, ranks, pooled, v, u, bias, upstream):
    whole = lambda *shape: pl.BlockSpec(shape, lambda g, s: (0,) * len(shape))
    return pl.pallas_call(
        backward_kernel,
        grid_spec=pltpu.PrefetchScalarGridSpec(
            num_scalar_prefetch=1,
            grid=(N_DP,),
            in_specs=[
                pl.BlockSpec((2, 1, WORDS, SAMPLES), lambda g, s: (0, g, 0, 0)),
                whole(2 * RANK, SAMPLES),
                whole(FEATS, SAMPLES),
                whole(FEATS, RANK),
                whole(FEATS, RANK),
                whole(FEATS, 1),
                whole(FEATS, SAMPLES),
            ],
            out_specs=[
                whole(FEATS, SAMPLES),
                pl.BlockSpec((1, OUT_ROWS, STEP_ROWS), lambda g, s: (jnp.minimum(g, 7), 0, 0)),
                pl.BlockSpec((1, OUT_ROWS, STEP_ROWS), lambda g, s: (jnp.maximum(g - 8, 0), 0, 0)),
            ],
            scratch_shapes=[
                pltpu.VMEM((2, FEATS, SAMPLES), bf16),
                pltpu.VMEM((N_DP * GRAD_ROWS, 2 * RANK), f32),
            ],
        ),
        out_shape=[
            jax.ShapeDtypeStruct((FEATS, SAMPLES), bf16),
            jax.ShapeDtypeStruct((8, OUT_ROWS, STEP_ROWS), bf16),
            jax.ShapeDtypeStruct((8, OUT_ROWS, STEP_ROWS), bf16),
        ],
        compiler_params=pltpu.CompilerParams(vmem_limit_bytes=VMEM),
        name="cross_and_row_grads",
    )(scalars, words, ranks, pooled, v, u, bias, upstream)


def exchange(x, axes):
    return lax.all_to_all(x, axes, 0, 0, tiled=True)


def spread(x, axes, count):
    return exchange(jnp.broadcast_to(x, (count,) + x.shape), axes)


def to_other_core(x):
    return lax.ppermute(x, "core", [(0, 1), (1, 0)])


def in_order(own, other, core):
    first = jnp.where(core == 0, own, other)
    second = jnp.where(core == 0, other, own)
    return jnp.stack([first, second], axis=1)


def body(rows_in, accum, bag_ids, cross_v, cross_u, cross_bias, upstream):
    block = lax.axis_index("row")
    core = lax.axis_index("core")
    part = lax.axis_index(DP_OUTER) * 2 + core
    table_a = (block * FEATS) // WIDTH
    table_b = jnp.minimum(table_a + 1, TABLES - 1)
    n_a = jnp.minimum(FEATS, WIDTH * (table_a + 1) - FEATS * block)

    my_rows = lax.dynamic_slice(rows_in, (0, part * PART, 0), (TABLES, PART, WIDTH))
    my_accum = lax.dynamic_slice(accum, (0, part * PART), (TABLES, PART))

    packed = my_rows.transpose(1, 0, 2).reshape(PART, N_ROW, FEATS).transpose(1, 0, 2)
    mine = exchange(packed, "row").reshape(STEP_ROWS, FEATS).T
    own = spread(mine, DP_OUTER, 8)
    other = to_other_core(own)

    upstream_t = upstream.T
    scalars = jnp.stack([table_a, table_b, core, n_a]).astype(jnp.int32)
    pooled, words, rank_parts = forward(
        scalars, bag_ids.transpose(1, 2, 0), own, other, cross_v, cross_u, upstream_t
    )

    gathered = exchange(rank_parts.reshape(N_ROW, 16, SAMPLES), "row")
    ranks = spread(jnp.sum(gathered.astype(f32), axis=0).astype(bf16), "row", N_ROW).reshape(2 * RANK, SAMPLES)

    scalars = jnp.stack([core, n_a]).astype(jnp.int32)
    crossed, own, other = backward(
        scalars, words, ranks, pooled, cross_v, cross_u, cross_bias.reshape(FEATS, 1), upstream_t
    )

    chip_sum = (own.astype(f32) + to_other_core(other).astype(f32)).astype(bf16)
    sums = jnp.sum(exchange(chip_sum, DP_OUTER).astype(f32), axis=0)
    row_grad = sums[:FEATS].astype(bf16).T.reshape(N_ROW, PART, FEATS)
    row_grad = exchange(row_grad, "row").transpose(1, 0, 2).reshape(PART, TABLES, WIDTH)
    row_grad = row_grad.transpose(1, 0, 2).astype(f32)

    accum_out = my_accum + jnp.mean(row_grad * row_grad, axis=2)
    scale = lax.rsqrt(accum_out + epsilon)
    rows_out = (my_rows.astype(f32) - learn_rate * row_grad * scale[:, :, None]).astype(bf16)

    high = accum_out.astype(bf16)
    rest = accum_out - high.astype(f32)
    middle = rest.astype(bf16)
    low = (rest - middle.astype(f32)).astype(bf16)
    accum_terms = jnp.stack([high, middle, low, jnp.zeros_like(low)]).reshape(13, WIDTH)
    cross_grads = sums[FEATS:].astype(bf16).reshape(32, WIDTH)
    result = jnp.concatenate([rows_out.reshape(TABLES * PART, WIDTH), accum_terms, cross_grads], axis=0)
    own = spread(result, DP_OUTER, 8)
    result = in_order(own, to_other_core(own), core)

    new_rows = result[:, :, :416].reshape(N_DP, TABLES, PART, WIDTH).transpose(1, 0, 2, 3).reshape(TABLES, ROWS, WIDTH)
    terms = result[:, :, 416:429].reshape(N_DP, 4, TABLES, PART).astype(f32)
    new_accum = (terms[:, 0] + terms[:, 1] + terms[:, 2]).transpose(1, 0, 2).reshape(TABLES, ROWS)
    cross_grads = result[:, :, 429:].reshape(N_DP * GRAD_ROWS, 2 * RANK).astype(f32)
    grad_u = cross_grads[:FEATS, :RANK]
    grad_v = cross_grads[:FEATS, RANK:]
    grad_bias = cross_grads[FEATS, :FEATS]
    return (crossed.T, new_rows, new_accum, grad_v, grad_u, grad_bias)


def solution(mesh):
    inner = Mesh(mesh.devices.reshape(4, 2, 2, N_ROW), DP_OUTER + ("core", "row"))
    dp = DP_OUTER + ("core",)
    return jax.shard_map(
        body,
        mesh=inner,
        in_specs=(
            P(None, "row", None),
            P(None, "row"),
            P(dp, None, None),
            P("row", None),
            P("row", None),
            P("row"),
            P(dp, "row"),
        ),
        out_specs=(
            P(dp, "row"),
            P(None, "row", None),
            P(None, "row"),
            P("row", None),
            P("row", None),
            P("row"),
        ),
        check_vma=False,
    )
```

```python
import jax
import jax.numpy as jnp
from jax import lax
from jax.experimental import pallas as pl
from jax.experimental.pallas import tpu as pltpu
from jax.sharding import Mesh
from jax.sharding import PartitionSpec as P

bf16 = jnp.bfloat16
f32 = jnp.float32
learn_rate = 0.3
epsilon = 1e-06

SAMPLES, TABLES, BAG, ROWS, WIDTH, FEATS, RANK = 512, 26, 8, 256, 128, 104, 256
N_ROW, N_DP, PART = 32, 16, 16
STEP_ROWS = N_ROW * PART
WORDS = STEP_ROWS // 8
GRAD_ROWS = 8
OUT_ROWS = FEATS + GRAD_ROWS
DP_OUTER = ("x_hi", "y")
ROW_AXES = ("z", "x_lo")
ROW_ALL = ("x_lo", "z")
BLOCK_OF = [(i & 1) * 16 + (i >> 1) for i in range(N_ROW)]
CHUNK = TABLES * PART + 16 + 32
VMEM = 40 << 20

NT_DIMS = (((1,), (1,)), ((), ()))
TN_DIMS = (((0,), (0,)), ((), ()))


def part_of(outer, core):
    return (outer & 3) * 4 + (outer >> 2) * 2 + core


def pieces(table):
    found = []
    for block in range(N_ROW):
        low = max(table * WIDTH, block * FEATS)
        high = min((table + 1) * WIDTH, (block + 1) * FEATS)
        if low < high:
            found.append((block, low - block * FEATS, high - block * FEATS))
    return found


def pack_kernel(scalars, rows, mine, packed):
    mine[...] = rows[...]
    for device, block in enumerate(BLOCK_OF):
        first = block * FEATS // WIDTH
        start = block * FEATS - first * WIDTH
        cut = rows[first][:, start:].astype(f32)
        if cut.shape[1] < FEATS:
            cut = jnp.concatenate([cut, rows[first + 1][:, : FEATS - cut.shape[1]].astype(f32)], axis=1)
        packed[device] = cut[:, :FEATS].astype(bf16)


def pack(scalars, rows):
    return pl.pallas_call(
        pack_kernel,
        grid_spec=pltpu.PrefetchScalarGridSpec(
            num_scalar_prefetch=1,
            grid=(1,),
            in_specs=[pl.BlockSpec((TABLES, PART, WIDTH), lambda g, s: (0, s[0], 0))],
            out_specs=[
                pl.BlockSpec((TABLES, PART, WIDTH), lambda g, s: (0, 0, 0)),
                pl.BlockSpec((N_ROW, PART, FEATS), lambda g, s: (0, 0, 0)),
            ],
        ),
        out_shape=[
            jax.ShapeDtypeStruct((TABLES, PART, WIDTH), bf16),
            jax.ShapeDtypeStruct((N_ROW, PART, FEATS), bf16),
        ],
        compiler_params=pltpu.CompilerParams(vmem_limit_bytes=VMEM),
        name="pack_rows",
    )(scalars, rows)


def adagrad_kernel(grads, rows, accum, cross_grads, out):
    table_lane = lax.broadcasted_iota(jnp.int32, (PART, WIDTH), 1)
    accum_in = accum[...]
    accum_out = jnp.zeros((PART, WIDTH), f32)
    device_of = {block: device for device, block in enumerate(BLOCK_OF)}
    for table in range(TABLES):
        cuts = [grads[device_of[block]].astype(f32)[:, low:high] for block, low, high in pieces(table)]
        grad = jnp.concatenate(cuts, axis=1)
        total = accum_in[:, table : table + 1] + jnp.mean(grad * grad, axis=1, keepdims=True)
        step = learn_rate * grad * lax.rsqrt(total + epsilon)
        new = (rows[table].astype(f32) - step).astype(bf16)
        for copy in range(8):
            out[copy, table * PART : (table + 1) * PART, :] = new
        accum_out = jnp.where(table_lane == table, total, accum_out)
    high = accum_out.astype(bf16).astype(f32)
    rest = accum_out - high
    middle = rest.astype(bf16).astype(f32)
    low = rest - middle
    terms = jnp.concatenate(
        [high[:, :32], middle[:, :32], low[:, :32], jnp.zeros((PART, 32), f32)], axis=1
    ).astype(bf16)
    wide = cross_grads[...]
    wide = jnp.concatenate([wide[:, lane : lane + WIDTH] for lane in range(0, 2 * RANK, WIDTH)], axis=0).astype(bf16)
    for copy in range(8):
        out[copy, TABLES * PART : TABLES * PART + PART, :] = terms
        out[copy, TABLES * PART + PART :, :] = wide


def adagrad(grads, rows, accum, cross_grads):
    return pl.pallas_call(
        adagrad_kernel,
        out_shape=jax.ShapeDtypeStruct((8, CHUNK, WIDTH), bf16),
        compiler_params=pltpu.CompilerParams(vmem_limit_bytes=VMEM),
        name="adagrad",
    )(grads, rows, accum, cross_grads)


def unpack_kernel(scalars, own, other, rows_out, accum_out, grad_v, grad_u, grad_bias, accums, cross_grads):
    for outer in range(8):
        for turn, source in enumerate((own, other)):
            part = part_of(outer, turn ^ scalars[0])
            rows_out[:, pl.ds(part, 1)] = source[outer, : TABLES * PART].reshape(TABLES, 1, PART, WIDTH)
            terms = source[outer, TABLES * PART : TABLES * PART + PART].astype(f32)
            total = terms[:, :32] + terms[:, 32:64] + terms[:, 64:96]
            accums[pl.ds(pl.multiple_of(part * PART, PART), PART), :] = jnp.concatenate(
                [total, jnp.zeros((PART, WIDTH - 32), f32)], axis=1
            )
            wide = source[outer, TABLES * PART + PART :].astype(f32)
            at = pl.multiple_of(part * GRAD_ROWS, GRAD_ROWS)
            for i in range(4):
                cross_grads[pl.ds(at, GRAD_ROWS), i * WIDTH : (i + 1) * WIDTH] = wide[i * 8 : (i + 1) * 8]
    accum_out[...] = accums[...].T[:TABLES]
    grad_u[...] = cross_grads[:FEATS, :RANK]
    grad_v[...] = cross_grads[:FEATS, RANK:]
    grad_bias[...] = cross_grads[FEATS : FEATS + 8, :WIDTH]


def unpack(scalars, own, other):
    whole = lambda *shape: pl.BlockSpec(shape, lambda g, s: (0,) * len(shape))
    shapes = [
        ((TABLES, N_DP, PART, WIDTH), bf16),
        ((TABLES, ROWS), f32),
        ((FEATS, RANK), f32),
        ((FEATS, RANK), f32),
        ((8, WIDTH), f32),
    ]
    return pl.pallas_call(
        unpack_kernel,
        grid_spec=pltpu.PrefetchScalarGridSpec(
            num_scalar_prefetch=1,
            grid=(1,),
            in_specs=[whole(8, CHUNK, WIDTH), whole(8, CHUNK, WIDTH)],
            out_specs=[whole(*shape) for shape, _ in shapes],
            scratch_shapes=[
                pltpu.VMEM((ROWS, WIDTH), f32),
                pltpu.VMEM((N_DP * GRAD_ROWS, 2 * RANK), f32),
            ],
        ),
        out_shape=[jax.ShapeDtypeStruct(shape, kind) for shape, kind in shapes],
        compiler_params=pltpu.CompilerParams(vmem_limit_bytes=VMEM),
        name="unpack",
    )(scalars, own, other)


def counts_of(words):
    columns = []
    for lane in range(0, SAMPLES, 128):
        blocks = []
        for group in range(0, WORDS, 8):
            word = words[group : group + 8, lane : lane + 128]
            digits = [lax.shift_right_logical(word, jnp.int32(4 * j)) & 15 for j in range(8)]
            blocks.append(jnp.concatenate(digits, axis=0).astype(f32).astype(bf16))
        columns.append(jnp.concatenate(blocks, axis=0))
    return jnp.concatenate(columns, axis=1)


def words_of(place):
    inside = (place >= 0) & (place < STEP_ROWS)
    word = jnp.where(inside, ((place >> 6) << 3) | (place & 7), -1)
    unit = jnp.left_shift(jnp.int32(1), ((place >> 3) & 7) * 4)
    columns = []
    for lane in range(0, SAMPLES, 128):
        slots = lax.broadcasted_iota(jnp.int32, (WORDS, 128), 0)
        total = jnp.zeros((WORDS, 128), jnp.int32)
        for k in range(BAG):
            here = word[k : k + 1, lane : lane + 128] == slots
            total = total + jnp.where(here, unit[k : k + 1, lane : lane + 128], 0)
        columns.append(total)
    return jnp.concatenate(columns, axis=1)


def forward_kernel(
    scalars, ids_a, ids_b, own, other, v, u, upstream, pooled_out, words_out, ranks_out, places, total
):
    step = pl.program_id(0)
    core = scalars[2]

    @pl.when(step == 0)
    def _():
        total[...] = jnp.zeros_like(total)
        for table, ids in enumerate((ids_a, ids_b)):
            row = ids[0]
            part = (row >> 4) & 15
            turn = (part & 1) ^ core
            outer = (((part >> 1) & 1) << 2) | (part >> 2)
            device = (((row >> 8) & 15) << 1) | (row >> 12)
            places[table] = turn * 4096 + outer * 512 + device * 16 + (row & 15)

    rows = jnp.where(step < 8, own[0].astype(f32), other[0].astype(f32)).astype(bf16)
    for table in range(2):
        words = words_of(places[table] - step * STEP_ROWS)
        words_out[table, 0] = words
        total[table] += jnp.dot(rows, counts_of(words), preferred_element_type=f32)

    @pl.when(step == N_DP - 1)
    def _():
        feature = lax.broadcasted_iota(jnp.int32, (FEATS, SAMPLES), 0)
        pooled = jnp.where(feature < scalars[3], total[0], total[1]).astype(bf16)
        pooled_out[...] = pooled
        gate_grad = (upstream[...].astype(f32) * pooled.astype(f32)).astype(bf16)
        ranks_out[:RANK] = lax.dot_general(v[...], pooled, TN_DIMS, preferred_element_type=f32).astype(bf16)
        ranks_out[RANK:] = lax.dot_general(u[...], gate_grad, TN_DIMS, preferred_element_type=f32).astype(bf16)


def forward(scalars, ids, own, other, v, u, upstream):
    whole = lambda *shape: pl.BlockSpec(shape, lambda g, s: (0,) * len(shape))
    return pl.pallas_call(
        forward_kernel,
        grid_spec=pltpu.PrefetchScalarGridSpec(
            num_scalar_prefetch=1,
            grid=(N_DP,),
            in_specs=[
                pl.BlockSpec((1, BAG, SAMPLES), lambda g, s: (s[0], 0, 0)),
                pl.BlockSpec((1, BAG, SAMPLES), lambda g, s: (s[1], 0, 0)),
                pl.BlockSpec((1, FEATS, STEP_ROWS), lambda g, s: (jnp.minimum(g, 7), 0, 0)),
                pl.BlockSpec((1, FEATS, STEP_ROWS), lambda g, s: (jnp.maximum(g - 8, 0), 0, 0)),
                whole(FEATS, RANK),
                whole(FEATS, RANK),
                whole(FEATS, SAMPLES),
            ],
            out_specs=[
                whole(FEATS, SAMPLES),
                pl.BlockSpec((2, 1, WORDS, SAMPLES), lambda g, s: (0, g, 0, 0)),
                whole(2 * RANK, SAMPLES),
            ],
            scratch_shapes=[
                pltpu.VMEM((2, BAG, SAMPLES), jnp.int32),
                pltpu.VMEM((2, FEATS, SAMPLES), f32),
            ],
        ),
        out_shape=[
            jax.ShapeDtypeStruct((FEATS, SAMPLES), bf16),
            pltpu.HBM((2, N_DP, WORDS, SAMPLES), jnp.int32),
            jax.ShapeDtypeStruct((2 * RANK, SAMPLES), bf16),
        ],
        compiler_params=pltpu.CompilerParams(vmem_limit_bytes=VMEM),
        name="bags_and_ranks",
    )(scalars, ids, ids, own, other, v, u, upstream)


def backward_kernel(
    scalars, words, ranks, pooled_in, v, u, bias, upstream_in, crossed_out, own_out, other_out, grads, cross_grads
):
    step = pl.program_id(0)

    @pl.when(step == 0)
    def _():
        rank = ranks[:RANK]
        rank_grad = ranks[RANK:]
        pooled_bf = pooled_in[...]
        pooled = pooled_bf.astype(f32)
        upstream = upstream_in[...].astype(f32)
        gate = jnp.dot(u[...], rank, preferred_element_type=f32) + bias[...]
        crossed_out[...] = (pooled * gate + pooled).astype(bf16)
        back = jnp.dot(v[...], rank_grad, preferred_element_type=f32)
        grad = (upstream * (gate + 1.0) + back).astype(bf16).astype(f32)
        feature = lax.broadcasted_iota(jnp.int32, (FEATS, SAMPLES), 0)
        grads[0] = jnp.where(feature < scalars[1], grad, 0.0).astype(bf16)
        grads[1] = jnp.where(feature < scalars[1], 0.0, grad).astype(bf16)
        gate_grad = upstream * pooled
        gate_bf = gate_grad.astype(bf16)
        gate_rest = (gate_grad - gate_bf.astype(f32)).astype(bf16)
        cross_grads[...] = jnp.zeros_like(cross_grads)
        cross_grads[:FEATS, :RANK] = lax.dot_general(gate_bf, rank, NT_DIMS, preferred_element_type=f32)
        cross_grads[:FEATS, RANK:] = lax.dot_general(pooled_bf, rank_grad, NT_DIMS, preferred_element_type=f32)
        ones = jnp.ones((16, SAMPLES), bf16)
        bias_sum = lax.dot_general(ones, gate_bf, NT_DIMS, preferred_element_type=f32) + lax.dot_general(
            ones, gate_rest, NT_DIMS, preferred_element_type=f32
        )
        cross_grads[FEATS : FEATS + 8, :FEATS] = bias_sum[:8]

    turn = step // 8
    part = part_of(step - 8 * turn, turn ^ scalars[0])
    result = lax.dot_general(grads[0], counts_of(words[0, 0]), NT_DIMS, preferred_element_type=f32)
    result = result + lax.dot_general(grads[1], counts_of(words[1, 0]), NT_DIMS, preferred_element_type=f32)
    extra = cross_grads[pl.ds(pl.multiple_of(part * GRAD_ROWS, GRAD_ROWS), GRAD_ROWS), :]
    block = jnp.concatenate([result, extra], axis=0).astype(bf16)

    @pl.when(turn == 0)
    def _():
        own_out[0] = block

    @pl.when(turn == 1)
    def _():
        other_out[0] = block


def backward(scalars, words, ranks, pooled, v, u, bias, upstream):
    whole = lambda *shape: pl.BlockSpec(shape, lambda g, s: (0,) * len(shape))
    return pl.pallas_call(
        backward_kernel,
        grid_spec=pltpu.PrefetchScalarGridSpec(
            num_scalar_prefetch=1,
            grid=(N_DP,),
            in_specs=[
                pl.BlockSpec((2, 1, WORDS, SAMPLES), lambda g, s: (0, g, 0, 0)),
                whole(2 * RANK, SAMPLES),
                whole(FEATS, SAMPLES),
                whole(FEATS, RANK),
                whole(FEATS, RANK),
                whole(FEATS, 1),
                whole(FEATS, SAMPLES),
            ],
            out_specs=[
                whole(FEATS, SAMPLES),
                pl.BlockSpec((1, OUT_ROWS, STEP_ROWS), lambda g, s: (jnp.minimum(g, 7), 0, 0)),
                pl.BlockSpec((1, OUT_ROWS, STEP_ROWS), lambda g, s: (jnp.maximum(g - 8, 0), 0, 0)),
            ],
            scratch_shapes=[
                pltpu.VMEM((2, FEATS, SAMPLES), bf16),
                pltpu.VMEM((N_DP * GRAD_ROWS, 2 * RANK), f32),
            ],
        ),
        out_shape=[
            jax.ShapeDtypeStruct((FEATS, SAMPLES), bf16),
            jax.ShapeDtypeStruct((8, OUT_ROWS, STEP_ROWS), bf16),
            jax.ShapeDtypeStruct((8, OUT_ROWS, STEP_ROWS), bf16),
        ],
        compiler_params=pltpu.CompilerParams(vmem_limit_bytes=VMEM),
        name="cross_and_row_grads",
    )(scalars, words, ranks, pooled, v, u, bias, upstream)


def exchange(x, axes):
    return lax.all_to_all(x, axes, 0, 0, tiled=True)


def spread(x, axes, count):
    return exchange(jnp.broadcast_to(x, (count,) + x.shape), axes)


def to_other_core(x):
    return lax.ppermute(x, "core", [(0, 1), (1, 0)])


def body(rows_in, accum, bag_ids, cross_v, cross_u, cross_bias, upstream):
    block = lax.axis_index("x_lo") * 16 + lax.axis_index("z")
    core = lax.axis_index("core")
    part = part_of(lax.axis_index(DP_OUTER), core)
    table_a = (block * FEATS) // WIDTH
    table_b = jnp.minimum(table_a + 1, TABLES - 1)
    n_a = jnp.minimum(FEATS, WIDTH * (table_a + 1) - FEATS * block)

    my_rows, packed = pack(jnp.stack([part]).astype(jnp.int32), rows_in)
    mine = exchange(packed, ROW_AXES).reshape(STEP_ROWS, FEATS).T
    own = spread(mine, DP_OUTER, 8)
    other = to_other_core(own)

    upstream_t = upstream.T
    scalars = jnp.stack([table_a, table_b, core, n_a]).astype(jnp.int32)
    pooled, words, rank_parts = forward(
        scalars, bag_ids.transpose(1, 2, 0), own, other, cross_v, cross_u, upstream_t
    )

    gathered = exchange(rank_parts.reshape(N_ROW, 16, SAMPLES), ROW_ALL)
    ranks = spread(jnp.sum(gathered.astype(f32), axis=0).astype(bf16), ROW_ALL, N_ROW).reshape(2 * RANK, SAMPLES)

    scalars = jnp.stack([core, n_a]).astype(jnp.int32)
    crossed, own, other = backward(
        scalars, words, ranks, pooled, cross_v, cross_u, cross_bias.reshape(FEATS, 1), upstream_t
    )

    chip_sum = (own.astype(f32) + to_other_core(other).astype(f32)).astype(bf16)
    sums = jnp.sum(exchange(chip_sum, DP_OUTER).astype(f32), axis=0)
    row_grad = exchange(sums[:FEATS].astype(bf16).T.reshape(N_ROW, PART, FEATS), ROW_AXES)
    my_accum = lax.dynamic_slice(accum, (0, part * PART), (TABLES, PART)).T

    own = exchange(adagrad(row_grad, my_rows, my_accum, sums[FEATS:]), DP_OUTER)
    new_rows, new_accum, grad_v, grad_u, grad_bias = unpack(
        jnp.stack([core]).astype(jnp.int32), own, to_other_core(own)
    )
    return (crossed.T, new_rows.reshape(TABLES, ROWS, WIDTH), new_accum, grad_v, grad_u, grad_bias[0, :FEATS])


def solution(mesh):
    inner = Mesh(mesh.devices.reshape(4, 2, 2, 2, 16), ("y", "x_hi", "core", "x_lo", "z"))
    dp = ("y", "x_hi", "core")
    row = ROW_ALL
    return jax.shard_map(
        body,
        mesh=inner,
        in_specs=(
            P(None, row, None),
            P(None, row),
            P(dp, None, None),
            P(row, None),
            P(row, None),
            P(row),
            P(dp, row),
        ),
        out_specs=(
            P(dp, row),
            P(None, row, None),
            P(None, row),
            P(row, None),
            P(row, None),
            P(row),
        ),
        check_vma=False,
    )
```

```python
import jax
import jax.numpy as jnp
from jax import lax
from jax.experimental import pallas as pl
from jax.experimental.pallas import tpu as pltpu
from jax.sharding import Mesh
from jax.sharding import PartitionSpec as P

bf16 = jnp.bfloat16
f32 = jnp.float32
learn_rate = 0.3
epsilon = 1e-06

SAMPLES, TABLES, BAG, ROWS, WIDTH, FEATS, RANK = 512, 26, 8, 256, 128, 104, 256
N_ROW, N_DP, PART = 32, 16, 16
STEP_ROWS = N_ROW * PART
WORDS = STEP_ROWS // 8
HALF = SAMPLES // 2
GRAD_ROWS = 8
OUT_ROWS = FEATS + GRAD_ROWS
DP_OUTER = ("x_hi", "y")
ROW_AXES = ("z", "x_lo")
ROW_ALL = ("x_lo", "z")
BLOCK_OF = [(i & 1) * 16 + (i >> 1) for i in range(N_ROW)]
CHUNK = TABLES * PART + 16 + 32
VMEM = 40 << 20

NT_DIMS = (((1,), (1,)), ((), ()))
TN_DIMS = (((0,), (0,)), ((), ()))


def part_of(outer, core):
    return (outer & 3) * 4 + (outer >> 2) * 2 + core


def pieces(table):
    found = []
    for block in range(N_ROW):
        low = max(table * WIDTH, block * FEATS)
        high = min((table + 1) * WIDTH, (block + 1) * FEATS)
        if low < high:
            found.append((block, low - block * FEATS, high - block * FEATS))
    return found


def pack_kernel(scalars, rows, mine, packed):
    mine[...] = rows[...]
    for device, block in enumerate(BLOCK_OF):
        first = block * FEATS // WIDTH
        start = block * FEATS - first * WIDTH
        cut = rows[first][:, start:].astype(f32)
        if cut.shape[1] < FEATS:
            cut = jnp.concatenate([cut, rows[first + 1][:, : FEATS - cut.shape[1]].astype(f32)], axis=1)
        packed[device] = cut[:, :FEATS].astype(bf16)


def pack(scalars, rows):
    return pl.pallas_call(
        pack_kernel,
        grid_spec=pltpu.PrefetchScalarGridSpec(
            num_scalar_prefetch=1,
            grid=(1,),
            in_specs=[pl.BlockSpec((TABLES, PART, WIDTH), lambda g, s: (0, s[0], 0))],
            out_specs=[
                pl.BlockSpec((TABLES, PART, WIDTH), lambda g, s: (0, 0, 0)),
                pl.BlockSpec((N_ROW, PART, FEATS), lambda g, s: (0, 0, 0)),
            ],
        ),
        out_shape=[
            jax.ShapeDtypeStruct((TABLES, PART, WIDTH), bf16),
            jax.ShapeDtypeStruct((N_ROW, PART, FEATS), bf16),
        ],
        name="pack_rows",
    )(scalars, rows)


def adagrad_kernel(grads, rows, accum, cross_grads, out):
    table_lane = lax.broadcasted_iota(jnp.int32, (PART, WIDTH), 1)
    accum_in = accum[...]
    accum_out = jnp.zeros((PART, WIDTH), f32)
    device_of = {block: device for device, block in enumerate(BLOCK_OF)}
    for table in range(TABLES):
        cuts = [grads[device_of[block]].astype(f32)[:, low:high] for block, low, high in pieces(table)]
        grad = jnp.concatenate(cuts, axis=1)
        total = accum_in[:, table : table + 1] + jnp.mean(grad * grad, axis=1, keepdims=True)
        step = learn_rate * grad * lax.rsqrt(total + epsilon)
        new = (rows[table].astype(f32) - step).astype(bf16)
        for copy in range(8):
            out[copy, table * PART : (table + 1) * PART, :] = new
        accum_out = jnp.where(table_lane == table, total, accum_out)
    high = accum_out.astype(bf16).astype(f32)
    rest = accum_out - high
    middle = rest.astype(bf16).astype(f32)
    low = rest - middle
    terms = jnp.concatenate(
        [high[:, :32], middle[:, :32], low[:, :32], jnp.zeros((PART, 32), f32)], axis=1
    ).astype(bf16)
    wide = cross_grads[...]
    wide = jnp.concatenate([wide[:, lane : lane + WIDTH] for lane in range(0, 2 * RANK, WIDTH)], axis=0).astype(bf16)
    for copy in range(8):
        out[copy, TABLES * PART : TABLES * PART + PART, :] = terms
        out[copy, TABLES * PART + PART :, :] = wide


def adagrad(grads, rows, accum, cross_grads):
    return pl.pallas_call(
        adagrad_kernel,
        out_shape=jax.ShapeDtypeStruct((8, CHUNK, WIDTH), bf16),
        compiler_params=pltpu.CompilerParams(vmem_limit_bytes=VMEM),
        name="adagrad",
    )(grads, rows, accum, cross_grads)


def unpack_kernel(scalars, own, other, rows_out, accum_out, grad_v, grad_u, grad_bias, accums, cross_grads):
    for outer in range(8):
        for turn, source in enumerate((own, other)):
            part = part_of(outer, turn ^ scalars[0])
            rows_out[:, pl.ds(part, 1)] = source[outer, : TABLES * PART].reshape(TABLES, 1, PART, WIDTH)
            terms = source[outer, TABLES * PART : TABLES * PART + PART].astype(f32)
            total = terms[:, :32] + terms[:, 32:64] + terms[:, 64:96]
            accums[pl.ds(pl.multiple_of(part * PART, PART), PART), :] = jnp.concatenate(
                [total, jnp.zeros((PART, WIDTH - 32), f32)], axis=1
            )
            wide = source[outer, TABLES * PART + PART :].astype(f32)
            at = pl.multiple_of(part * GRAD_ROWS, GRAD_ROWS)
            for i in range(4):
                cross_grads[pl.ds(at, GRAD_ROWS), i * WIDTH : (i + 1) * WIDTH] = wide[i * 8 : (i + 1) * 8]
    accum_out[...] = accums[...].T[:TABLES]
    grad_u[...] = cross_grads[:FEATS, :RANK]
    grad_v[...] = cross_grads[:FEATS, RANK:]
    grad_bias[...] = cross_grads[FEATS : FEATS + 8, :WIDTH]


def unpack(scalars, own, other):
    whole = lambda *shape: pl.BlockSpec(shape, lambda g, s: (0,) * len(shape))
    shapes = [
        ((TABLES, N_DP, PART, WIDTH), bf16),
        ((TABLES, ROWS), f32),
        ((FEATS, RANK), f32),
        ((FEATS, RANK), f32),
        ((8, WIDTH), f32),
    ]
    return pl.pallas_call(
        unpack_kernel,
        grid_spec=pltpu.PrefetchScalarGridSpec(
            num_scalar_prefetch=1,
            grid=(1,),
            in_specs=[whole(8, CHUNK, WIDTH), whole(8, CHUNK, WIDTH)],
            out_specs=[whole(*shape) for shape, _ in shapes],
            scratch_shapes=[
                pltpu.VMEM((ROWS, WIDTH), f32),
                pltpu.VMEM((N_DP * GRAD_ROWS, 2 * RANK), f32),
            ],
        ),
        out_shape=[jax.ShapeDtypeStruct(shape, kind) for shape, kind in shapes],
        compiler_params=pltpu.CompilerParams(vmem_limit_bytes=VMEM),
        name="unpack",
    )(scalars, own, other)


def counts_of(words):
    columns = []
    for lane in range(0, words.shape[1], 128):
        blocks = []
        for group in range(0, WORDS, 8):
            word = words[group : group + 8, lane : lane + 128]
            digits = [lax.shift_right_logical(word, jnp.int32(4 * j)) & 15 for j in range(8)]
            blocks.append(jnp.concatenate(digits, axis=0).astype(f32).astype(bf16))
        columns.append(jnp.concatenate(blocks, axis=0))
    return jnp.concatenate(columns, axis=1)


def words_of(place):
    inside = (place >= 0) & (place < STEP_ROWS)
    word = jnp.where(inside, ((place >> 6) << 3) | (place & 7), -1)
    unit = jnp.left_shift(jnp.int32(1), ((place >> 3) & 7) * 4)
    columns = []
    for lane in range(0, SAMPLES, 128):
        slots = lax.broadcasted_iota(jnp.int32, (WORDS, 128), 0)
        total = jnp.zeros((WORDS, 128), jnp.int32)
        for k in range(BAG):
            here = word[k : k + 1, lane : lane + 128] == slots
            total = total + jnp.where(here, unit[k : k + 1, lane : lane + 128], 0)
        columns.append(total)
    return jnp.concatenate(columns, axis=1)


def whole(*shape):
    return pl.BlockSpec(shape, lambda g, s: (0,) * len(shape))


def words_kernel(scalars, ids_a, ids_b, words, places):
    step = pl.program_id(0)

    @pl.when(step == 0)
    def _():
        for table, ids in enumerate((ids_a, ids_b)):
            row = ids[0]
            part = (row >> 4) & 15
            turn = (part & 1) ^ scalars[2]
            outer = (((part >> 1) & 1) << 2) | (part >> 2)
            device = (((row >> 8) & 15) << 1) | (row >> 12)
            places[table] = turn * 4096 + outer * 512 + device * 16 + (row & 15)

    for table in range(2):
        for turn in range(2):
            words[table, turn, 0] = words_of(places[table] - (turn * 8 + step) * STEP_ROWS)


def bag_words(scalars, ids):
    return pl.pallas_call(
        words_kernel,
        grid_spec=pltpu.PrefetchScalarGridSpec(
            num_scalar_prefetch=1,
            grid=(8,),
            in_specs=[
                pl.BlockSpec((1, BAG, SAMPLES), lambda g, s: (s[0], 0, 0)),
                pl.BlockSpec((1, BAG, SAMPLES), lambda g, s: (s[1], 0, 0)),
            ],
            out_specs=[pl.BlockSpec((2, 2, 1, WORDS, SAMPLES), lambda g, s: (0, 0, g, 0, 0))],
            scratch_shapes=[pltpu.VMEM((2, BAG, SAMPLES), jnp.int32)],
        ),
        out_shape=[jax.ShapeDtypeStruct((2, 2, 8, WORDS, SAMPLES), jnp.int32)],
        compiler_params=pltpu.CompilerParams(vmem_limit_bytes=VMEM),
        cost_estimate=pl.CostEstimate(flops=1 << 28, bytes_accessed=5 << 20, transcendentals=0),
        name="bag_words",
    )(scalars, ids, ids)[0]


WORD_BLOCK = pl.BlockSpec((2, 2, 1, WORDS, HALF), lambda g, s: (0, 0, g, 0, s[0]))
HALF_BLOCK = pl.BlockSpec((FEATS, HALF), lambda g, s: (0, s[0]))
KERNEL_COST = pl.CostEstimate(flops=1 << 32, bytes_accessed=5 << 20, transcendentals=0)


def forward_kernel(scalars, words, own, other, v, u, upstream, pooled_out, ranks_out, total):
    step = pl.program_id(0)

    @pl.when(step == 0)
    def _():
        total[...] = jnp.zeros_like(total)

    for table in range(2):
        total[table] += jnp.dot(own[0], counts_of(words[table, 0, 0]), preferred_element_type=f32) + jnp.dot(
            other[0], counts_of(words[table, 1, 0]), preferred_element_type=f32
        )

    @pl.when(step == 7)
    def _():
        feature = lax.broadcasted_iota(jnp.int32, (FEATS, HALF), 0)
        pooled = jnp.where(feature < scalars[1], total[0], total[1]).astype(bf16)
        pooled_out[...] = pooled
        gate_grad = (upstream[...].astype(f32) * pooled.astype(f32)).astype(bf16)
        ranks_out[:RANK] = lax.dot_general(v[...], pooled, TN_DIMS, preferred_element_type=f32).astype(bf16)
        ranks_out[RANK:] = lax.dot_general(u[...], gate_grad, TN_DIMS, preferred_element_type=f32).astype(bf16)


def forward(scalars, words, own, other, v, u, upstream):
    return pl.pallas_call(
        forward_kernel,
        grid_spec=pltpu.PrefetchScalarGridSpec(
            num_scalar_prefetch=1,
            grid=(8,),
            in_specs=[
                WORD_BLOCK,
                pl.BlockSpec((1, FEATS, STEP_ROWS), lambda g, s: (g, 0, 0)),
                pl.BlockSpec((1, FEATS, STEP_ROWS), lambda g, s: (g, 0, 0)),
                whole(FEATS, RANK),
                whole(FEATS, RANK),
                HALF_BLOCK,
            ],
            out_specs=[whole(FEATS, HALF), whole(2 * RANK, HALF)],
            scratch_shapes=[pltpu.VMEM((2, FEATS, HALF), f32)],
        ),
        out_shape=[
            jax.ShapeDtypeStruct((FEATS, HALF), bf16),
            jax.ShapeDtypeStruct((2 * RANK, HALF), bf16),
        ],
        compiler_params=pltpu.CompilerParams(vmem_limit_bytes=VMEM),
        cost_estimate=KERNEL_COST,
        name="bags_and_ranks",
    )(scalars, words, own, other, v, u, upstream)


def backward_kernel(scalars, words, ranks, pooled_in, v, u, bias, upstream_in, *refs):
    if len(refs) == 5:
        sums_in = None
        crossed_out, own_out, other_out, grads, cross_grads = refs
    else:
        own_in, other_in, _, crossed_out, own_out, other_out, grads, cross_grads = refs
        sums_in = (own_in, other_in)
    step = pl.program_id(0)

    @pl.when(step == 0)
    def _():
        rank = ranks[:RANK]
        rank_grad = ranks[RANK:]
        pooled_bf = pooled_in[...]
        pooled = pooled_bf.astype(f32)
        upstream = upstream_in[...].astype(f32)
        gate = jnp.dot(u[...], rank, preferred_element_type=f32) + bias[...]
        crossed_out[...] = (pooled * gate + pooled).astype(bf16)
        back = jnp.dot(v[...], rank_grad, preferred_element_type=f32)
        grad = (upstream * (gate + 1.0) + back).astype(bf16).astype(f32)
        feature = lax.broadcasted_iota(jnp.int32, (FEATS, HALF), 0)
        grads[0] = jnp.where(feature < scalars[1], grad, 0.0).astype(bf16)
        grads[1] = jnp.where(feature < scalars[1], 0.0, grad).astype(bf16)
        gate_grad = upstream * pooled
        gate_bf = gate_grad.astype(bf16)
        gate_rest = (gate_grad - gate_bf.astype(f32)).astype(bf16)
        cross_grads[...] = jnp.zeros_like(cross_grads)
        cross_grads[:FEATS, :RANK] = lax.dot_general(gate_bf, rank, NT_DIMS, preferred_element_type=f32)
        cross_grads[:FEATS, RANK:] = lax.dot_general(pooled_bf, rank_grad, NT_DIMS, preferred_element_type=f32)
        ones = jnp.ones((16, HALF), bf16)
        bias_sum = lax.dot_general(ones, gate_bf, NT_DIMS, preferred_element_type=f32) + lax.dot_general(
            ones, gate_rest, NT_DIMS, preferred_element_type=f32
        )
        cross_grads[FEATS : FEATS + 8, :FEATS] = bias_sum[:8]

    for turn, out in enumerate((own_out, other_out)):
        part = part_of(step, turn ^ scalars[2])
        result = lax.dot_general(grads[0], counts_of(words[0, turn, 0]), NT_DIMS, preferred_element_type=f32)
        result = result + lax.dot_general(
            grads[1], counts_of(words[1, turn, 0]), NT_DIMS, preferred_element_type=f32
        )
        extra = cross_grads[pl.ds(pl.multiple_of(part * GRAD_ROWS, GRAD_ROWS), GRAD_ROWS), :]
        block = jnp.concatenate([result, extra], axis=0)
        if sums_in is not None:
            block = block + sums_in[turn][0]
        out[0] = block.astype(out.dtype)


def backward(scalars, words, ranks, pooled, v, u, bias, upstream, before=None):
    sums = pl.BlockSpec((1, OUT_ROWS, STEP_ROWS), lambda g, s: (g, 0, 0))
    kind = f32 if before is None else bf16
    operands = [scalars, words, ranks, pooled, v, u, bias, upstream]
    in_specs = [
        WORD_BLOCK,
        whole(2 * RANK, HALF),
        whole(FEATS, HALF),
        whole(FEATS, RANK),
        whole(FEATS, RANK),
        whole(FEATS, 1),
        HALF_BLOCK,
    ]
    aliases = {}
    if before is not None:
        crossed, own, other = before
        operands += [own, other, crossed]
        in_specs += [sums, sums, pl.BlockSpec(memory_space=pl.ANY)]
        aliases = {len(operands) - 1: 0}
    return pl.pallas_call(
        backward_kernel,
        grid_spec=pltpu.PrefetchScalarGridSpec(
            num_scalar_prefetch=1,
            grid=(8,),
            in_specs=in_specs,
            out_specs=[HALF_BLOCK, sums, sums],
            scratch_shapes=[
                pltpu.VMEM((2, FEATS, HALF), bf16),
                pltpu.VMEM((N_DP * GRAD_ROWS, 2 * RANK), f32),
            ],
        ),
        out_shape=[
            jax.ShapeDtypeStruct((FEATS, SAMPLES), bf16),
            jax.ShapeDtypeStruct((8, OUT_ROWS, STEP_ROWS), kind),
            jax.ShapeDtypeStruct((8, OUT_ROWS, STEP_ROWS), kind),
        ],
        input_output_aliases=aliases,
        compiler_params=pltpu.CompilerParams(vmem_limit_bytes=VMEM),
        cost_estimate=KERNEL_COST,
        name="cross_and_row_grads",
    )(*operands)


def exchange(x, axes):
    return lax.all_to_all(x, axes, 0, 0, tiled=True)


def spread(x, axes, count):
    return exchange(jnp.broadcast_to(x, (count,) + x.shape), axes)


def swap(x, axis):
    return lax.ppermute(x, axis, [(0, 1), (1, 0)])


def to_other_core(x):
    return swap(x, "core")


def body(rows_in, accum, bag_ids, cross_v, cross_u, cross_bias, upstream):
    block = lax.axis_index("x_lo") * 16 + lax.axis_index("z")
    core = lax.axis_index("core")
    part = part_of(lax.axis_index(DP_OUTER), core)
    table_a = (block * FEATS) // WIDTH
    table_b = jnp.minimum(table_a + 1, TABLES - 1)
    n_a = jnp.minimum(FEATS, WIDTH * (table_a + 1) - FEATS * block)

    my_rows, packed = pack(jnp.stack([part]).astype(jnp.int32), rows_in)
    mine = exchange(packed, ROW_AXES).reshape(STEP_ROWS, FEATS).T
    own = spread(mine, DP_OUTER, 8)
    other = to_other_core(own)

    upstream_t = upstream.T
    keep = lax.axis_index("x_lo")
    scalars = jnp.stack([table_a, table_b, core]).astype(jnp.int32)
    words = bag_words(scalars, bag_ids.transpose(1, 2, 0))
    at_keep = jnp.stack([keep, n_a, core]).astype(jnp.int32)
    at_sent = jnp.stack([1 - keep, n_a, core]).astype(jnp.int32)
    sent_pooled, sent_ranks = forward(at_sent, words, own, other, cross_v, cross_u, upstream_t)
    kept_pooled, kept_ranks = forward(at_keep, words, own, other, cross_v, cross_u, upstream_t)

    kept_ranks = (kept_ranks.astype(f32) + swap(sent_ranks, "x_lo").astype(f32)).astype(bf16)
    gathered = exchange(kept_ranks.reshape(16, 32, HALF), "z")
    ranks = spread(jnp.sum(gathered.astype(f32), axis=0).astype(bf16), "z", 16).reshape(2 * RANK, HALF)
    sent_ranks = swap(ranks, "x_lo")

    bias = cross_bias.reshape(FEATS, 1)
    half = backward(at_keep, words, ranks, kept_pooled, cross_v, cross_u, bias, upstream_t)
    crossed, own, other = backward(
        at_sent, words, sent_ranks, sent_pooled, cross_v, cross_u, bias, upstream_t, half
    )

    chip_sum = (own.astype(f32) + to_other_core(other).astype(f32)).astype(bf16)
    sums = jnp.sum(exchange(chip_sum, DP_OUTER).astype(f32), axis=0)
    row_grad = exchange(sums[:FEATS].astype(bf16).T.reshape(N_ROW, PART, FEATS), ROW_AXES)
    my_accum = lax.dynamic_slice(accum, (0, part * PART), (TABLES, PART)).T

    own = exchange(adagrad(row_grad, my_rows, my_accum, sums[FEATS:]), DP_OUTER)
    new_rows, new_accum, grad_v, grad_u, grad_bias = unpack(
        jnp.stack([core]).astype(jnp.int32), own, to_other_core(own)
    )
    return (crossed.T, new_rows.reshape(TABLES, ROWS, WIDTH), new_accum, grad_v, grad_u, grad_bias[0, :FEATS])


def solution(mesh):
    inner = Mesh(mesh.devices.reshape(4, 2, 2, 2, 16), ("y", "x_hi", "core", "x_lo", "z"))
    dp = ("y", "x_hi", "core")
    row = ROW_ALL
    return jax.shard_map(
        body,
        mesh=inner,
        in_specs=(
            P(None, row, None),
            P(None, row),
            P(dp, None, None),
            P(row, None),
            P(row, None),
            P(row),
            P(dp, row),
        ),
        out_specs=(
            P(dp, row),
            P(None, row, None),
            P(None, row),
            P(row, None),
            P(row, None),
            P(row),
        ),
        check_vma=False,
    )
```

```python
import functools

import jax
import jax.numpy as jnp
from jax import lax
from jax.experimental import pallas as pl
from jax.experimental.pallas import tpu as pltpu
from jax.sharding import Mesh
from jax.sharding import PartitionSpec as P

bf16 = jnp.bfloat16
f32 = jnp.float32
learn_rate = 0.3
epsilon = 1e-06

SAMPLES, TABLES, BAG, ROWS, WIDTH, FEATS, RANK = 512, 26, 8, 256, 128, 104, 256
N_ROW, N_DP, PART = 32, 16, 16
STEP_ROWS = N_ROW * PART
WORDS = STEP_ROWS // 8
HALF = SAMPLES // 2
GRAD_ROWS = 8
OUT_ROWS = FEATS + GRAD_ROWS
DP_OUTER = ("x_hi", "y")
ROW_AXES = ("z", "x_lo")
ROW_ALL = ("x_lo", "z")
BLOCK_OF = [(i & 1) * 16 + (i >> 1) for i in range(N_ROW)]
CHUNK = TABLES * PART + 16 + 32
UNROLL = 2
VMEM = 16 << 20

NT_DIMS = (((1,), (1,)), ((), ()))
TN_DIMS = (((0,), (0,)), ((), ()))


def part_of(outer, core):
    return (outer & 3) * 4 + (outer >> 2) * 2 + core


def pieces(table):
    found = []
    for block in range(N_ROW):
        low = max(table * WIDTH, block * FEATS)
        high = min((table + 1) * WIDTH, (block + 1) * FEATS)
        if low < high:
            found.append((block, low - block * FEATS, high - block * FEATS))
    return found


def pack_kernel(scalars, rows, mine, packed):
    mine[...] = rows[...]
    for device, block in enumerate(BLOCK_OF):
        first = block * FEATS // WIDTH
        start = block * FEATS - first * WIDTH
        cut = rows[first][:, start:].astype(f32)
        if cut.shape[1] < FEATS:
            cut = jnp.concatenate([cut, rows[first + 1][:, : FEATS - cut.shape[1]].astype(f32)], axis=1)
        packed[device] = cut[:, :FEATS].astype(bf16)


def pack(scalars, rows):
    return pl.pallas_call(
        pack_kernel,
        grid_spec=pltpu.PrefetchScalarGridSpec(
            num_scalar_prefetch=1,
            grid=(1,),
            in_specs=[pl.BlockSpec((TABLES, PART, WIDTH), lambda g, s: (0, s[0], 0))],
            out_specs=[
                pl.BlockSpec((TABLES, PART, WIDTH), lambda g, s: (0, 0, 0)),
                pl.BlockSpec((N_ROW, PART, FEATS), lambda g, s: (0, 0, 0)),
            ],
        ),
        out_shape=[
            jax.ShapeDtypeStruct((TABLES, PART, WIDTH), bf16),
            jax.ShapeDtypeStruct((N_ROW, PART, FEATS), bf16),
        ],
        name="pack_rows",
    )(scalars, rows)


def adagrad_kernel(grads, rows, accum, cross_grads, out):
    table_lane = lax.broadcasted_iota(jnp.int32, (PART, WIDTH), 1)
    accum_in = accum[...]
    accum_out = jnp.zeros((PART, WIDTH), f32)
    device_of = {block: device for device, block in enumerate(BLOCK_OF)}
    for table in range(TABLES):
        cuts = [grads[device_of[block]].astype(f32)[:, low:high] for block, low, high in pieces(table)]
        grad = jnp.concatenate(cuts, axis=1)
        total = accum_in[:, table : table + 1] + jnp.mean(grad * grad, axis=1, keepdims=True)
        step = learn_rate * grad * lax.rsqrt(total + epsilon)
        new = (rows[table].astype(f32) - step).astype(bf16)
        for copy in range(8):
            out[copy, table * PART : (table + 1) * PART, :] = new
        accum_out = jnp.where(table_lane == table, total, accum_out)
    high = accum_out.astype(bf16).astype(f32)
    rest = accum_out - high
    middle = rest.astype(bf16).astype(f32)
    low = rest - middle
    terms = jnp.concatenate(
        [high[:, :32], middle[:, :32], low[:, :32], jnp.zeros((PART, 32), f32)], axis=1
    ).astype(bf16)
    wide = cross_grads[...]
    wide = jnp.concatenate([wide[:, lane : lane + WIDTH] for lane in range(0, 2 * RANK, WIDTH)], axis=0).astype(bf16)
    for copy in range(8):
        out[copy, TABLES * PART : TABLES * PART + PART, :] = terms
        out[copy, TABLES * PART + PART :, :] = wide


def adagrad(grads, rows, accum, cross_grads):
    return pl.pallas_call(
        adagrad_kernel,
        out_shape=jax.ShapeDtypeStruct((8, CHUNK, WIDTH), bf16),
        compiler_params=pltpu.CompilerParams(vmem_limit_bytes=VMEM),
        name="adagrad",
    )(grads, rows, accum, cross_grads)


def unpack_kernel(scalars, own, other, rows_out, accum_out, grad_v, grad_u, grad_bias, accums, cross_grads):
    for outer in range(8):
        for turn, source in enumerate((own, other)):
            part = part_of(outer, turn ^ scalars[0])
            rows_out[:, pl.ds(part, 1)] = source[outer, : TABLES * PART].reshape(TABLES, 1, PART, WIDTH)
            terms = source[outer, TABLES * PART : TABLES * PART + PART].astype(f32)
            total = terms[:, :32] + terms[:, 32:64] + terms[:, 64:96]
            accums[pl.ds(pl.multiple_of(part * PART, PART), PART), :] = jnp.concatenate(
                [total, jnp.zeros((PART, WIDTH - 32), f32)], axis=1
            )
            wide = source[outer, TABLES * PART + PART :].astype(f32)
            at = pl.multiple_of(part * GRAD_ROWS, GRAD_ROWS)
            for i in range(4):
                cross_grads[pl.ds(at, GRAD_ROWS), i * WIDTH : (i + 1) * WIDTH] = wide[i * 8 : (i + 1) * 8]
    accum_out[...] = accums[...].T[:TABLES]
    grad_u[...] = cross_grads[:FEATS, :RANK]
    grad_v[...] = cross_grads[:FEATS, RANK:]
    grad_bias[...] = cross_grads[FEATS, :FEATS]


def unpack(scalars, own, other):
    whole = lambda *shape: pl.BlockSpec(shape, lambda g, s: (0,) * len(shape))
    shapes = [
        ((TABLES, N_DP, PART, WIDTH), bf16),
        ((TABLES, ROWS), f32),
        ((FEATS, RANK), f32),
        ((FEATS, RANK), f32),
        ((FEATS,), f32),
    ]
    return pl.pallas_call(
        unpack_kernel,
        grid_spec=pltpu.PrefetchScalarGridSpec(
            num_scalar_prefetch=1,
            grid=(1,),
            in_specs=[whole(8, CHUNK, WIDTH), whole(8, CHUNK, WIDTH)],
            out_specs=[whole(*shape) for shape, _ in shapes],
            scratch_shapes=[
                pltpu.VMEM((ROWS, WIDTH), f32),
                pltpu.VMEM((N_DP * GRAD_ROWS, 2 * RANK), f32),
            ],
        ),
        out_shape=[jax.ShapeDtypeStruct(shape, kind) for shape, kind in shapes],
        compiler_params=pltpu.CompilerParams(vmem_limit_bytes=VMEM),
        name="unpack",
    )(scalars, own, other)


def counts_of(words, scaled=False):
    columns = []
    for lane in range(0, words.shape[1], 128):
        blocks = []
        for group in range(0, WORDS, 8):
            word = words[group : group + 8, lane : lane + 128]
            if scaled:
                digits = [word & jnp.int32(15 << (4 * j)) for j in range(7)]
            else:
                digits = [lax.shift_right_logical(word, jnp.int32(4 * j)) & 15 for j in range(7)]
            digits.append(lax.shift_right_logical(word, jnp.int32(28)))
            blocks.append(jnp.concatenate(digits, axis=0).astype(f32).astype(bf16))
        columns.append(jnp.concatenate(blocks, axis=0))
    return jnp.concatenate(columns, axis=1)


def words_of(place):
    inside = (place >= 0) & (place < STEP_ROWS)
    word = jnp.where(inside, ((place >> 6) << 3) | (place & 7), -1)
    unit = jnp.left_shift(jnp.int32(1), ((place >> 3) & 7) * 4)
    columns = []
    for lane in range(0, place.shape[1], 128):
        slots = lax.broadcasted_iota(jnp.int32, (WORDS, 128), 0)
        total = jnp.zeros((WORDS, 128), jnp.int32)
        for k in range(BAG):
            here = word[k : k + 1, lane : lane + 128] == slots
            total = total + jnp.where(here, unit[k : k + 1, lane : lane + 128], 0)
        columns.append(total)
    return jnp.concatenate(columns, axis=1)


def whole(*shape):
    return pl.BlockSpec(shape, lambda g, s: (0,) * len(shape))


def words_kernel(scalars, *refs):
    ids, outs, places = refs[:4], refs[4:6], refs[6]
    step = pl.program_id(0)

    @pl.when(step == 0)
    def _():
        for i in range(4):
            row = ids[i][0]
            part = (row >> 4) & 15
            turn = (part & 1) ^ scalars[2]
            outer = (((part >> 1) & 1) << 2) | (part >> 2)
            device = (((row >> 8) & 15) << 1) | (row >> 12)
            places[i] = turn * 4096 + outer * 512 + device * 16 + (row & 15)

    for half, words in enumerate(outs):
        for table in range(2):
            for turn in range(2):
                words[table, turn, 0] = words_of(places[2 * half + table] - (turn * 8 + step) * STEP_ROWS)


def bag_words(scalars, ids):
    return pl.pallas_call(
        words_kernel,
        grid_spec=pltpu.PrefetchScalarGridSpec(
            num_scalar_prefetch=1,
            grid=(8,),
            in_specs=[
                pl.BlockSpec((1, BAG, HALF), lambda g, s: (s[0], 0, s[3])),
                pl.BlockSpec((1, BAG, HALF), lambda g, s: (s[1], 0, s[3])),
                pl.BlockSpec((1, BAG, HALF), lambda g, s: (s[0], 0, 1 - s[3])),
                pl.BlockSpec((1, BAG, HALF), lambda g, s: (s[1], 0, 1 - s[3])),
            ],
            out_specs=[pl.BlockSpec((2, 2, 1, WORDS, HALF), lambda g, s: (0, 0, g, 0, 0))] * 2,
            scratch_shapes=[pltpu.VMEM((4, BAG, HALF), jnp.int32)],
        ),
        out_shape=[jax.ShapeDtypeStruct((2, 2, 8, WORDS, HALF), jnp.int32)] * 2,
        compiler_params=pltpu.CompilerParams(vmem_limit_bytes=VMEM),
        cost_estimate=pl.CostEstimate(flops=1 << 28, bytes_accessed=5 << 20, transcendentals=0),
        name="bag_words",
    )(scalars, ids, ids, ids, ids)


HALF_BLOCK = pl.BlockSpec((FEATS, HALF), lambda g, s: (0, s[0]))
KERNEL_COST = pl.CostEstimate(flops=1 << 32, bytes_accessed=5 << 20, transcendentals=0)


def words_block(first_turn, turns):
    block = first_turn if turns == 1 else 0
    return pl.BlockSpec((2, turns, UNROLL, WORDS, HALF), lambda g, s: (0, block, g, 0, 0))


def call(kernel, name, steps, operands, in_specs, out_specs, out_shape, scratch_shapes=(), aliases=None):
    return pl.pallas_call(
        kernel,
        grid_spec=pltpu.PrefetchScalarGridSpec(
            num_scalar_prefetch=1,
            grid=(steps,),
            in_specs=in_specs,
            out_specs=out_specs,
            scratch_shapes=list(scratch_shapes),
        ),
        out_shape=out_shape,
        input_output_aliases=aliases or {},
        compiler_params=pltpu.CompilerParams(vmem_limit_bytes=VMEM),
        cost_estimate=KERNEL_COST,
        name=name,
    )(*operands)


def forward_kernel(turns, last, scalars, words, *refs):
    step = pl.program_id(0)
    rows, refs = refs[:turns], refs[turns:]
    if last:
        *before, pooled_out, total = refs
    else:
        before, total = refs[:-1], refs[-1]

    @pl.when(step == 0)
    def _():
        total[...] = before[0][...] if before else jnp.zeros_like(total)

    for i in range(UNROLL):
        for table in range(2):
            for turn, source in enumerate(rows):
                counts = counts_of(words[table, turn, i], scaled=True)
                total[table] += jnp.dot(source[i], counts, preferred_element_type=f32)

    if last:

        @pl.when(step == 8 // UNROLL - 1)
        def _():
            feature = lax.broadcasted_iota(jnp.int32, (FEATS, HALF), 0)
            pooled_out[...] = jnp.where(feature < scalars[1], total[0], total[1]).astype(bf16)


def forward(scalars, words, rows, first_turn, before=None, last=True):
    turns = len(rows)
    operands = [scalars, words, *rows]
    in_specs = [words_block(first_turn, turns)]
    in_specs += [pl.BlockSpec((UNROLL, FEATS, STEP_ROWS), lambda g, s: (g, 0, 0))] * turns
    if before is not None:
        operands.append(before)
        in_specs.append(whole(2, FEATS, HALF))
    if last:
        out_specs, out_shape = whole(FEATS, HALF), jax.ShapeDtypeStruct((FEATS, HALF), bf16)
        scratch = [pltpu.VMEM((2, FEATS, HALF), f32)]
    else:
        out_specs, out_shape, scratch = whole(2, FEATS, HALF), jax.ShapeDtypeStruct((2, FEATS, HALF), f32), []
    kernel = functools.partial(forward_kernel, turns, last)
    return call(kernel, "bags", 8 // UNROLL, operands, in_specs, out_specs, out_shape, scratch)


def ranks_kernel(scalars, pooled_a, pooled_b, v_a, u_a, upstream_a, v_b, u_b, upstream_b, ranks):
    rank = jnp.zeros((RANK, HALF), f32)
    rank_grad = jnp.zeros((RANK, HALF), f32)
    for pooled_in, v, u, upstream in ((pooled_a, v_a, u_a, upstream_a), (pooled_b, v_b, u_b, upstream_b)):
        pooled = pooled_in[...]
        gate_grad = (upstream[...].astype(f32) * pooled.astype(f32)).astype(bf16)
        rank += lax.dot_general(v[...], pooled, TN_DIMS, preferred_element_type=f32)
        rank_grad += lax.dot_general(u[...], gate_grad, TN_DIMS, preferred_element_type=f32)
    ranks[:RANK] = rank.astype(bf16)
    ranks[RANK:] = rank_grad.astype(bf16)


def rank_terms(scalars, pooled, partner_pooled, v, u, upstream, partner):
    side = [pl.BlockSpec((FEATS, HALF), lambda g, s, i=i: (0, i)) for i in range(3)]
    return call(
        ranks_kernel,
        "rank_terms",
        1,
        [scalars, pooled, partner_pooled, v, u, upstream, partner, partner, partner],
        [whole(FEATS, HALF), whole(FEATS, HALF), whole(FEATS, RANK), whole(FEATS, RANK), HALF_BLOCK, *side],
        whole(2 * RANK, HALF),
        jax.ShapeDtypeStruct((2 * RANK, HALF), bf16),
    )


def cross_layer(scalars, ranks, pooled_in, v, u, bias, upstream_in, crossed_out, grads, cross_grads):
    rank = ranks[:RANK]
    rank_grad = ranks[RANK:]
    pooled_bf = pooled_in[...]
    pooled = pooled_bf.astype(f32)
    upstream = upstream_in[...].astype(f32)
    gate = jnp.dot(u[...], rank, preferred_element_type=f32) + bias[...]
    crossed_out[...] = (pooled * gate + pooled).astype(bf16)
    back = jnp.dot(v[...], rank_grad, preferred_element_type=f32)
    grad = (upstream * (gate + 1.0) + back).astype(bf16).astype(f32)
    feature = lax.broadcasted_iota(jnp.int32, (FEATS, HALF), 0)
    grads[0] = jnp.where(feature < scalars[1], grad, 0.0).astype(bf16)
    grads[1] = jnp.where(feature < scalars[1], 0.0, grad).astype(bf16)
    gate_grad = upstream * pooled
    gate_bf = gate_grad.astype(bf16)
    gate_rest = (gate_grad - gate_bf.astype(f32)).astype(bf16)
    cross_grads[...] = jnp.zeros_like(cross_grads)
    cross_grads[:FEATS, :RANK] = lax.dot_general(gate_bf, rank, NT_DIMS, preferred_element_type=f32)
    cross_grads[:FEATS, RANK:] = lax.dot_general(pooled_bf, rank_grad, NT_DIMS, preferred_element_type=f32)
    ones = jnp.ones((16, HALF), bf16)
    bias_sum = lax.dot_general(ones, gate_bf, NT_DIMS, preferred_element_type=f32) + lax.dot_general(
        ones, gate_rest, NT_DIMS, preferred_element_type=f32
    )
    cross_grads[FEATS : FEATS + 8, :FEATS] = bias_sum[:8]


def row_grads(scalars, turns, words, grads, cross_grads, before, outs):
    step = pl.program_id(0)
    for i in range(UNROLL):
        for n, turn in enumerate(turns):
            part = part_of(step * UNROLL + i, turn ^ scalars[2])
            result = lax.dot_general(grads[0], counts_of(words[0, n, i]), NT_DIMS, preferred_element_type=f32)
            result += lax.dot_general(grads[1], counts_of(words[1, n, i]), NT_DIMS, preferred_element_type=f32)
            extra = cross_grads[pl.ds(pl.multiple_of(part * GRAD_ROWS, GRAD_ROWS), GRAD_ROWS), :]
            block = jnp.concatenate([result, extra], axis=0)
            if before is not None:
                block = block + before[i]
            outs[n][i] = block.astype(outs[n].dtype)


def backward_kernel(turns, scalars, words, ranks, pooled, v, u, bias, upstream, *refs):
    if len(turns) == 2:
        before = None
        crossed, own, other, grads, cross_grads = refs
        outs = (own, other)
    else:
        before, _, crossed, grads, cross_grads, other = refs
        outs = (other,)

    @pl.when(pl.program_id(0) == 0)
    def _():
        cross_layer(scalars, ranks, pooled, v, u, bias, upstream, crossed, grads, cross_grads)

    row_grads(scalars, turns, words, grads, cross_grads, before, outs)


def rest_kernel(scalars, words, grads, cross_grads, before, own):
    row_grads(scalars, (0,), words, grads, cross_grads, before, (own,))


SUMS_BLOCK = pl.BlockSpec((UNROLL, OUT_ROWS, STEP_ROWS), lambda g, s: (g, 0, 0))
SUMS_SHAPE = (8, OUT_ROWS, STEP_ROWS)
CROSS_SPECS = [whole(2 * RANK, HALF), whole(FEATS, HALF), whole(FEATS, RANK), whole(FEATS, RANK), whole(FEATS, 1), HALF_BLOCK]
CROSSED = jax.ShapeDtypeStruct((FEATS, SAMPLES), bf16)
GRADS = (2, FEATS, HALF)
CROSS_GRADS = (N_DP * GRAD_ROWS, 2 * RANK)


def first_backward(scalars, words, *operands):
    return call(
        functools.partial(backward_kernel, (0, 1)),
        "cross_and_row_grads",
        8 // UNROLL,
        [scalars, words, *operands],
        [words_block(0, 2), *CROSS_SPECS],
        [HALF_BLOCK, SUMS_BLOCK, SUMS_BLOCK],
        [CROSSED, jax.ShapeDtypeStruct(SUMS_SHAPE, f32), jax.ShapeDtypeStruct(SUMS_SHAPE, f32)],
        [pltpu.VMEM(GRADS, bf16), pltpu.VMEM(CROSS_GRADS, f32)],
    )


def second_backward(scalars, words, *operands):
    return call(
        functools.partial(backward_kernel, (1,)),
        "cross_and_row_grads",
        8 // UNROLL,
        [scalars, words, *operands],
        [words_block(1, 1), *CROSS_SPECS, SUMS_BLOCK, pl.BlockSpec(memory_space=pl.ANY)],
        [HALF_BLOCK, whole(*GRADS), whole(*CROSS_GRADS), SUMS_BLOCK],
        [
            CROSSED,
            jax.ShapeDtypeStruct(GRADS, bf16),
            jax.ShapeDtypeStruct(CROSS_GRADS, f32),
            jax.ShapeDtypeStruct(SUMS_SHAPE, bf16),
        ],
        aliases={len(operands) + 1: 0},
    )


def rest_of_backward(scalars, words, grads, cross_grads, before):
    return call(
        rest_kernel,
        "row_grads",
        8 // UNROLL,
        [scalars, words, grads, cross_grads, before],
        [words_block(0, 1), whole(*GRADS), whole(*CROSS_GRADS), SUMS_BLOCK],
        SUMS_BLOCK,
        jax.ShapeDtypeStruct(SUMS_SHAPE, bf16),
    )


def exchange(x, axes):
    return lax.all_to_all(x, axes, 0, 0, tiled=True)


def spread(x, axes, count):
    return exchange(jnp.broadcast_to(x, (count,) + x.shape), axes)


def swap(x, axis):
    return lax.ppermute(x, axis, [(0, 1), (1, 0)])


def to_other_core(x):
    return swap(x, "core")


def body(rows_in, accum, bag_ids, cross_v, cross_u, cross_bias, upstream):
    block = lax.axis_index("x_lo") * 16 + lax.axis_index("z")
    core = lax.axis_index("core")
    part = part_of(lax.axis_index(DP_OUTER), core)
    table_a = (block * FEATS) // WIDTH
    table_b = jnp.minimum(table_a + 1, TABLES - 1)
    n_a = jnp.minimum(FEATS, WIDTH * (table_a + 1) - FEATS * block)

    upstream_t = upstream.T
    sent_upstream = lax.dynamic_slice(upstream_t, (0, (1 - lax.axis_index("x_lo")) * HALF), (FEATS, HALF))
    partner = swap(jnp.concatenate([cross_v, cross_u, sent_upstream], axis=1), "x_lo")

    my_rows, packed = pack(jnp.stack([part]).astype(jnp.int32), rows_in)
    mine = exchange(packed, ROW_AXES).reshape(STEP_ROWS, FEATS).T
    nibble = (jnp.arange(STEP_ROWS) >> 3) & 7
    mine = mine * jnp.where(nibble == 7, 1.0, jnp.exp2(-4.0 * nibble)).astype(bf16)
    mine, partner = lax.optimization_barrier((mine, partner))
    own = spread(mine, DP_OUTER, 8)
    keep = lax.axis_index("x_lo")
    scalars = jnp.stack([table_a, table_b, core, keep]).astype(jnp.int32)
    at_keep = jnp.stack([keep, n_a, core]).astype(jnp.int32)
    at_sent = jnp.stack([1 - keep, n_a, core]).astype(jnp.int32)
    kept_words, sent_words = bag_words(scalars, bag_ids.transpose(1, 2, 0))
    own, kept_words, sent_words = lax.optimization_barrier((own, kept_words, sent_words))
    other = to_other_core(own)

    sent_sums = forward(at_sent, sent_words, [own], 0, last=False)
    sent_pooled = forward(at_sent, sent_words, [other], 1, before=sent_sums)
    partner_pooled = swap(sent_pooled, "x_lo")
    kept_pooled = forward(at_keep, kept_words, [own, other], 0)

    terms = rank_terms(at_keep, kept_pooled, partner_pooled, cross_v, cross_u, upstream_t, partner)
    gathered = exchange(terms.reshape(16, 32, HALF), "z")
    ranks = spread(jnp.sum(gathered.astype(f32), axis=0).astype(bf16), "z", 16).reshape(2 * RANK, HALF)
    sent_ranks = swap(ranks, "x_lo")

    cross = (cross_v, cross_u, cross_bias.reshape(FEATS, 1), upstream_t)
    crossed, own, other = first_backward(at_keep, kept_words, ranks, kept_pooled, *cross)
    crossed, grads, cross_grads, other = second_backward(
        at_sent, sent_words, sent_ranks, sent_pooled, *cross, other, crossed
    )
    from_other = to_other_core(other)
    own = rest_of_backward(at_sent, sent_words, grads, cross_grads, own)

    chip_sum = (own.astype(f32) + from_other.astype(f32)).astype(bf16)
    sums = jnp.sum(exchange(chip_sum, DP_OUTER).astype(f32), axis=0)
    row_grad = exchange(sums[:FEATS].astype(bf16).T.reshape(N_ROW, PART, FEATS), ROW_AXES)
    my_accum = lax.dynamic_slice(accum, (0, part * PART), (TABLES, PART)).T

    own = exchange(adagrad(row_grad, my_rows, my_accum, sums[FEATS:]), DP_OUTER)
    new_rows, new_accum, grad_v, grad_u, grad_bias = unpack(
        jnp.stack([core]).astype(jnp.int32), own, to_other_core(own)
    )
    return (crossed.T, new_rows.reshape(TABLES, ROWS, WIDTH), new_accum, grad_v, grad_u, grad_bias)


def solution(mesh):
    inner = Mesh(mesh.devices.reshape(4, 2, 2, 2, 16), ("y", "x_hi", "core", "x_lo", "z"))
    dp = ("y", "x_hi", "core")
    row = ROW_ALL
    return jax.shard_map(
        body,
        mesh=inner,
        in_specs=(
            P(None, row, None),
            P(None, row),
            P(dp, None, None),
            P(row, None),
            P(row, None),
            P(row),
            P(dp, row),
        ),
        out_specs=(
            P(dp, row),
            P(None, row, None),
            P(None, row),
            P(row, None),
            P(row, None),
            P(row),
        ),
        check_vma=False,
    )
```

```python
import functools

import jax
import jax.numpy as jnp
from jax import lax
from jax.experimental import pallas as pl
from jax.experimental.pallas import tpu as pltpu
from jax.sharding import Mesh
from jax.sharding import PartitionSpec as P

bf16 = jnp.bfloat16
f32 = jnp.float32
learn_rate = 0.3
epsilon = 1e-06

SAMPLES, TABLES, BAG, ROWS, WIDTH, FEATS, RANK = 512, 26, 8, 256, 128, 104, 256
N_ROW, N_DP, PART = 32, 16, 16
STEP_ROWS = N_ROW * PART
WORDS = STEP_ROWS // 8
HALF = SAMPLES // 2
GRAD_ROWS = 8
OUT_ROWS = FEATS + GRAD_ROWS
DP_OUTER = ("x_hi", "y")
ROW_AXES = ("z", "x_lo")
ROW_ALL = ("x_lo", "z")
BLOCK_OF = [(i & 1) * 16 + (i >> 1) for i in range(N_ROW)]
CHUNK = TABLES * PART + 16 + 32
UNROLL = 2
VMEM = 16 << 20

NT_DIMS = (((1,), (1,)), ((), ()))
TN_DIMS = (((0,), (0,)), ((), ()))


def part_of(outer, core):
    return (outer & 3) * 4 + (outer >> 2) * 2 + core


def pieces(table):
    found = []
    for block in range(N_ROW):
        low = max(table * WIDTH, block * FEATS)
        high = min((table + 1) * WIDTH, (block + 1) * FEATS)
        if low < high:
            found.append((block, low - block * FEATS, high - block * FEATS))
    return found


def pack_kernel(scalars, rows, mine, packed):
    mine[...] = rows[...]
    for device, block in enumerate(BLOCK_OF):
        first = block * FEATS // WIDTH
        start = block * FEATS - first * WIDTH
        cut = rows[first][:, start:].astype(f32)
        if cut.shape[1] < FEATS:
            cut = jnp.concatenate([cut, rows[first + 1][:, : FEATS - cut.shape[1]].astype(f32)], axis=1)
        packed[device] = cut[:, :FEATS].astype(bf16)


def pack(scalars, rows):
    return pl.pallas_call(
        pack_kernel,
        grid_spec=pltpu.PrefetchScalarGridSpec(
            num_scalar_prefetch=1,
            grid=(1,),
            in_specs=[pl.BlockSpec((TABLES, PART, WIDTH), lambda g, s: (0, s[0], 0))],
            out_specs=[
                pl.BlockSpec((TABLES, PART, WIDTH), lambda g, s: (0, 0, 0)),
                pl.BlockSpec((N_ROW, PART, FEATS), lambda g, s: (0, 0, 0)),
            ],
        ),
        out_shape=[
            jax.ShapeDtypeStruct((TABLES, PART, WIDTH), bf16),
            jax.ShapeDtypeStruct((N_ROW, PART, FEATS), bf16),
        ],
        name="pack_rows",
    )(scalars, rows)


def adagrad_kernel(grads_in, rows, accum, cross_grads, out):
    device_of = {block: device for device, block in enumerate(BLOCK_OF)}
    grads = [
        jnp.concatenate([grads_in[device_of[block]].astype(f32)[:, low:high] for block, low, high in pieces(table)], axis=1)
        for table in range(TABLES)
    ]
    grad = jnp.concatenate(grads, axis=0)
    square = grad * grad
    high = square.astype(bf16)
    rest = (square - high.astype(f32)).astype(bf16)
    ones = jnp.ones((WIDTH, WIDTH), bf16)
    sums = jnp.dot(high, ones, preferred_element_type=f32) + jnp.dot(rest, ones, preferred_element_type=f32)
    total = accum[...] + sums * (1.0 / WIDTH)
    new = (rows[...].astype(f32) - learn_rate * grad * lax.rsqrt(total + epsilon)).astype(bf16)
    lane = lax.broadcasted_iota(jnp.int32, (PART, WIDTH), 1)
    accum_out = jnp.zeros((PART, WIDTH), f32)
    for table in range(TABLES):
        mine = total[table * PART : (table + 1) * PART]
        high = mine.astype(bf16).astype(f32)
        rest = mine - high
        middle = rest.astype(bf16).astype(f32)
        accum_out = jnp.where(lane == table, high, accum_out)
        accum_out = jnp.where(lane == table + 32, middle, accum_out)
        accum_out = jnp.where(lane == table + 64, rest - middle, accum_out)
    terms = accum_out.astype(bf16)
    wide = cross_grads[...]
    wide = jnp.concatenate([wide[:, at : at + WIDTH] for at in range(0, 2 * RANK, WIDTH)], axis=0).astype(bf16)
    for copy in range(8):
        out[copy, : TABLES * PART, :] = new
        out[copy, TABLES * PART : TABLES * PART + PART, :] = terms
        out[copy, TABLES * PART + PART :, :] = wide


def adagrad(grads, rows, accum, cross_grads):
    return pl.pallas_call(
        adagrad_kernel,
        out_shape=jax.ShapeDtypeStruct((8, CHUNK, WIDTH), bf16),
        compiler_params=pltpu.CompilerParams(vmem_limit_bytes=VMEM),
        name="adagrad",
    )(grads, rows, accum, cross_grads)


def unpack_kernel(scalars, own, other, rows_out, accum_out, grad_v, grad_u, grad_bias, accums, cross_grads):
    for outer in range(8):
        for turn, source in enumerate((own, other)):
            part = part_of(outer, turn ^ scalars[0])
            rows_out[:, pl.ds(part, 1)] = source[outer, : TABLES * PART].reshape(TABLES, 1, PART, WIDTH)
            terms = source[outer, TABLES * PART : TABLES * PART + PART].astype(f32)
            total = terms[:, :32] + terms[:, 32:64] + terms[:, 64:96]
            accums[pl.ds(pl.multiple_of(part * PART, PART), PART), :] = jnp.concatenate(
                [total, jnp.zeros((PART, WIDTH - 32), f32)], axis=1
            )
            wide = source[outer, TABLES * PART + PART :].astype(f32)
            at = pl.multiple_of(part * GRAD_ROWS, GRAD_ROWS)
            for i in range(4):
                cross_grads[pl.ds(at, GRAD_ROWS), i * WIDTH : (i + 1) * WIDTH] = wide[i * 8 : (i + 1) * 8]
    accum_out[...] = accums[...].T[:TABLES]
    grad_u[...] = cross_grads[:FEATS, :RANK]
    grad_v[...] = cross_grads[:FEATS, RANK:]
    grad_bias[...] = cross_grads[FEATS, :FEATS]


def unpack(scalars, own, other):
    shapes = [
        ((TABLES, N_DP, PART, WIDTH), bf16),
        ((TABLES, ROWS), f32),
        ((FEATS, RANK), f32),
        ((FEATS, RANK), f32),
        ((FEATS,), f32),
    ]
    return call(
        unpack_kernel,
        "unpack",
        scalars,
        (own, other),
        [jax.ShapeDtypeStruct(shape, kind) for shape, kind in shapes],
        [pltpu.VMEM((ROWS, WIDTH), f32), pltpu.VMEM((N_DP * GRAD_ROWS, 2 * RANK), f32)],
    )


def counts_of(words, scaled=False):
    columns = []
    for lane in range(0, words.shape[1], 128):
        blocks = []
        for group in range(0, WORDS, 8):
            word = words[group : group + 8, lane : lane + 128]
            if scaled:
                digits = [word & jnp.int32(15 << (4 * j)) for j in range(7)]
            else:
                digits = [lax.shift_right_logical(word, jnp.int32(4 * j)) & 15 for j in range(7)]
            digits.append(lax.shift_right_logical(word, jnp.int32(28)))
            blocks.append(jnp.concatenate(digits, axis=0).astype(f32).astype(bf16))
        columns.append(jnp.concatenate(blocks, axis=0))
    return jnp.concatenate(columns, axis=1)


def words_of(place):
    inside = (place >= 0) & (place < STEP_ROWS)
    word = jnp.where(inside, ((place >> 6) << 3) | (place & 7), -1)
    unit = jnp.left_shift(jnp.int32(1), ((place >> 3) & 7) * 4)
    columns = []
    for lane in range(0, place.shape[1], 128):
        slots = lax.broadcasted_iota(jnp.int32, (WORDS, 128), 0)
        total = jnp.zeros((WORDS, 128), jnp.int32)
        for k in range(BAG):
            here = word[k : k + 1, lane : lane + 128] == slots
            total = total + jnp.where(here, unit[k : k + 1, lane : lane + 128], 0)
        columns.append(total)
    return jnp.concatenate(columns, axis=1)


def whole(*shape):
    return pl.BlockSpec(shape, lambda g, s: (0,) * len(shape))


def words_kernel(scalars, *refs):
    ids, kept, sent, places = refs[:4], refs[4], refs[5:7], refs[7]
    step = pl.program_id(0)

    @pl.when(step == 0)
    def _():
        for i in range(4):
            row = ids[i][0]
            part = (row >> 4) & 15
            turn = (part & 1) ^ scalars[2]
            outer = (((part >> 1) & 1) << 2) | (part >> 2)
            device = (((row >> 8) & 15) << 1) | (row >> 12)
            places[i] = turn * 4096 + outer * 512 + device * 16 + (row & 15)

    for table in range(2):
        for turn in range(2):
            first = (turn * 8 + step) * STEP_ROWS
            kept[table, turn, 0] = words_of(places[table] - first)
            sent[turn][table, 0, 0] = words_of(places[2 + table] - first)


def bag_words(scalars, ids):
    return pl.pallas_call(
        words_kernel,
        grid_spec=pltpu.PrefetchScalarGridSpec(
            num_scalar_prefetch=1,
            grid=(8,),
            in_specs=[
                pl.BlockSpec((1, BAG, HALF), lambda g, s: (s[0], 0, s[3])),
                pl.BlockSpec((1, BAG, HALF), lambda g, s: (s[1], 0, s[3])),
                pl.BlockSpec((1, BAG, HALF), lambda g, s: (s[0], 0, 1 - s[3])),
                pl.BlockSpec((1, BAG, HALF), lambda g, s: (s[1], 0, 1 - s[3])),
            ],
            out_specs=[pl.BlockSpec((2, turns, 1, WORDS, HALF), lambda g, s: (0, 0, g, 0, 0)) for turns in (2, 1, 1)],
            scratch_shapes=[pltpu.VMEM((4, BAG, HALF), jnp.int32)],
        ),
        out_shape=[jax.ShapeDtypeStruct((2, turns, 8, WORDS, HALF), jnp.int32) for turns in (2, 1, 1)],
        compiler_params=pltpu.CompilerParams(vmem_limit_bytes=VMEM),
        cost_estimate=pl.CostEstimate(flops=1 << 28, bytes_accessed=5 << 20, transcendentals=0),
        name="bag_words",
    )(scalars, ids, ids, ids, ids)


KERNEL_COST = pl.CostEstimate(flops=1 << 32, bytes_accessed=5 << 20, transcendentals=0)


def call(kernel, name, scalars, operands, out_shape, scratch_shapes=()):
    return pl.pallas_call(
        kernel,
        in_specs=[pl.BlockSpec(memory_space=pltpu.SMEM)] + [pl.BlockSpec(memory_space=pltpu.VMEM)] * len(operands),
        out_shape=out_shape,
        scratch_shapes=list(scratch_shapes),
        compiler_params=pltpu.CompilerParams(vmem_limit_bytes=VMEM),
        cost_estimate=KERNEL_COST,
        name=name,
    )(scalars, *operands)


def half_of(scalars):
    return pl.ds(pl.multiple_of(scalars[0] * HALF, HALF), HALF)


def forward_kernel(turns, last, scalars, words, *refs):
    rows, refs = refs[:turns], refs[turns:]
    if last:
        *before, pooled_out, total = refs
    else:
        before, total = refs[:-1], refs[-1]
    total[...] = before[0][...] if before else jnp.zeros_like(total)

    @pl.loop(0, 8 // UNROLL)
    def _(step):
        for table in range(2):
            added = None
            for i in range(UNROLL):
                for turn, source in enumerate(rows):
                    counts = counts_of(words[table, turn, step * UNROLL + i], scaled=True)
                    term = jnp.dot(source[step * UNROLL + i], counts, preferred_element_type=f32)
                    added = term if added is None else added + term
            total[table] += added

    if last:
        feature = lax.broadcasted_iota(jnp.int32, (FEATS, HALF), 0)
        pooled_out[...] = jnp.where(feature < scalars[1], total[0], total[1]).astype(bf16)


def forward(scalars, words, rows, before=None, last=True):
    operands = [words, *rows] if before is None else [words, *rows, before]
    if last:
        out_shape, scratch = jax.ShapeDtypeStruct((FEATS, HALF), bf16), [pltpu.VMEM((2, FEATS, HALF), f32)]
    else:
        out_shape, scratch = jax.ShapeDtypeStruct((2, FEATS, HALF), f32), []
    return call(functools.partial(forward_kernel, len(rows), last), "bags", scalars, operands, out_shape, scratch)


def ranks_kernel(scalars, pooled_a, pooled_b, v_a, u_a, upstream_a, partner, ranks):
    rank = jnp.zeros((RANK, HALF), f32)
    rank_grad = jnp.zeros((RANK, HALF), f32)
    sides = (
        (pooled_a[...], v_a[...], u_a[...], upstream_a[:, half_of(scalars)]),
        (pooled_b[...], partner[:, :RANK], partner[:, RANK : 2 * RANK], partner[:, 2 * RANK :]),
    )
    for pooled, v, u, upstream in sides:
        gate_grad = (upstream.astype(f32) * pooled.astype(f32)).astype(bf16)
        rank += lax.dot_general(v, pooled, TN_DIMS, preferred_element_type=f32)
        rank_grad += lax.dot_general(u, gate_grad, TN_DIMS, preferred_element_type=f32)
    ranks[:RANK] = rank.astype(bf16)
    ranks[RANK:] = rank_grad.astype(bf16)


def rank_terms(scalars, *operands):
    return call(ranks_kernel, "rank_terms", scalars, operands, jax.ShapeDtypeStruct((2 * RANK, HALF), bf16))


def cross_layer(scalars, ranks, pooled_in, v, u, bias, upstream_in, grads, cross_grads):
    rank = ranks[:RANK]
    rank_grad = ranks[RANK:]
    pooled_bf = pooled_in[...]
    pooled = pooled_bf.astype(f32)
    upstream = upstream_in[:, half_of(scalars)].astype(f32)
    gate = jnp.dot(u[...], rank, preferred_element_type=f32) + bias[...]
    crossed = (pooled * gate + pooled).astype(bf16)
    back = jnp.dot(v[...], rank_grad, preferred_element_type=f32)
    grad = (upstream * (gate + 1.0) + back).astype(bf16).astype(f32)
    feature = lax.broadcasted_iota(jnp.int32, (FEATS, HALF), 0)
    grads[0] = jnp.where(feature < scalars[1], grad, 0.0).astype(bf16)
    grads[1] = jnp.where(feature < scalars[1], 0.0, grad).astype(bf16)
    gate_grad = upstream * pooled
    gate_bf = gate_grad.astype(bf16)
    gate_rest = (gate_grad - gate_bf.astype(f32)).astype(bf16)
    cross_grads[...] = jnp.zeros_like(cross_grads)
    cross_grads[:FEATS, :RANK] = lax.dot_general(gate_bf, rank, NT_DIMS, preferred_element_type=f32)
    cross_grads[:FEATS, RANK:] = lax.dot_general(pooled_bf, rank_grad, NT_DIMS, preferred_element_type=f32)
    ones = jnp.ones((16, HALF), bf16)
    bias_sum = lax.dot_general(ones, gate_bf, NT_DIMS, preferred_element_type=f32) + lax.dot_general(
        ones, gate_rest, NT_DIMS, preferred_element_type=f32
    )
    cross_grads[FEATS : FEATS + 8, :FEATS] = bias_sum[:8]
    return crossed


def row_grads(scalars, turns, words, grads, cross_grads, before, outs):
    @pl.loop(0, 8 // UNROLL)
    def _(step):
        for i in range(UNROLL):
            at = step * UNROLL + i
            for n, turn in enumerate(turns):
                part = part_of(at, turn ^ scalars[2])
                result = lax.dot_general(grads[0], counts_of(words[0, n, at]), NT_DIMS, preferred_element_type=f32)
                result += lax.dot_general(grads[1], counts_of(words[1, n, at]), NT_DIMS, preferred_element_type=f32)
                extra = cross_grads[pl.ds(pl.multiple_of(part * GRAD_ROWS, GRAD_ROWS), GRAD_ROWS), :]
                block = jnp.concatenate([result, extra], axis=0)
                if before is not None:
                    block = block + before[at]
                outs[n][at] = block.astype(outs[n].dtype)


def first_kernel(scalars, words, ranks, pooled, v, u, bias, upstream, crossed, own, other, grads, cross_grads):
    crossed[...] = cross_layer(scalars, ranks, pooled, v, u, bias, upstream, grads, cross_grads)
    row_grads(scalars, (0, 1), words, grads, cross_grads, None, (own, other))


def second_kernel(
    scalars, words, ranks, pooled, v, u, bias, upstream, before, first, crossed, grads, cross_grads, other
):
    mine = cross_layer(scalars, ranks, pooled, v, u, bias, upstream, grads, cross_grads)
    crossed[:, half_of(scalars)] = mine
    crossed[:, pl.ds(pl.multiple_of((1 - scalars[0]) * HALF, HALF), HALF)] = first[...]
    row_grads(scalars, (1,), words, grads, cross_grads, before, (other,))


def rest_kernel(scalars, words, grads, cross_grads, before, own):
    row_grads(scalars, (0,), words, grads, cross_grads, before, (own,))


SUMS = (8, OUT_ROWS, STEP_ROWS)
GRADS = (2, FEATS, HALF)
CROSS_GRADS = (N_DP * GRAD_ROWS, 2 * RANK)


def first_backward(scalars, *operands):
    return call(
        first_kernel,
        "cross_and_row_grads",
        scalars,
        operands,
        [jax.ShapeDtypeStruct((FEATS, HALF), bf16), jax.ShapeDtypeStruct(SUMS, f32), jax.ShapeDtypeStruct(SUMS, f32)],
        [pltpu.VMEM(GRADS, bf16), pltpu.VMEM(CROSS_GRADS, f32)],
    )


def second_backward(scalars, *operands):
    return call(
        second_kernel,
        "cross_and_row_grads",
        scalars,
        operands,
        [
            jax.ShapeDtypeStruct((FEATS, SAMPLES), bf16),
            jax.ShapeDtypeStruct(GRADS, bf16),
            jax.ShapeDtypeStruct(CROSS_GRADS, f32),
            jax.ShapeDtypeStruct(SUMS, bf16),
        ],
    )


def rest_of_backward(scalars, *operands):
    return call(rest_kernel, "row_grads", scalars, operands, jax.ShapeDtypeStruct(SUMS, bf16))


def exchange(x, axes):
    return lax.all_to_all(x, axes, 0, 0, tiled=True)


def spread(x, axes, count):
    return exchange(jnp.broadcast_to(x, (count,) + x.shape), axes)


def swap(x, axis):
    return lax.ppermute(x, axis, [(0, 1), (1, 0)])


def to_other_core(x):
    return swap(x, "core")


def body(rows_in, accum, bag_ids, cross_v, cross_u, cross_bias, upstream):
    block = lax.axis_index("x_lo") * 16 + lax.axis_index("z")
    core = lax.axis_index("core")
    part = part_of(lax.axis_index(DP_OUTER), core)
    table_a = (block * FEATS) // WIDTH
    table_b = jnp.minimum(table_a + 1, TABLES - 1)
    n_a = jnp.minimum(FEATS, WIDTH * (table_a + 1) - FEATS * block)

    upstream_t = upstream.T
    sent_upstream = lax.dynamic_slice(upstream_t, (0, (1 - lax.axis_index("x_lo")) * HALF), (FEATS, HALF))
    partner = swap(jnp.concatenate([cross_v, cross_u, sent_upstream], axis=1), "x_lo")

    my_rows, packed = pack(jnp.stack([part]).astype(jnp.int32), rows_in)
    mine = exchange(packed, ROW_AXES).reshape(STEP_ROWS, FEATS).T
    nibble = (jnp.arange(STEP_ROWS) >> 3) & 7
    mine = mine * jnp.where(nibble == 7, 1.0, jnp.exp2(-4.0 * nibble)).astype(bf16)
    mine, partner = lax.optimization_barrier((mine, partner))
    own = spread(mine, DP_OUTER, 8)
    keep = lax.axis_index("x_lo")
    scalars = jnp.stack([table_a, table_b, core, keep]).astype(jnp.int32)
    at_keep = jnp.stack([keep, n_a, core]).astype(jnp.int32)
    at_sent = jnp.stack([1 - keep, n_a, core]).astype(jnp.int32)
    words = bag_words(scalars, bag_ids.transpose(1, 2, 0))
    own, kept_words, own_words, other_words = lax.optimization_barrier((own, *words))
    other = to_other_core(own)

    sent_sums = forward(at_sent, own_words, [own], last=False)
    sent_pooled = forward(at_sent, other_words, [other], before=sent_sums)
    partner_pooled = swap(sent_pooled, "x_lo")
    kept_pooled = forward(at_keep, kept_words, [own, other])

    terms = rank_terms(at_keep, kept_pooled, partner_pooled, cross_v, cross_u, upstream_t, partner)
    gathered = exchange(terms.reshape(16, 32, HALF), "z")
    ranks = spread(jnp.sum(gathered.astype(f32), axis=0).astype(bf16), "z", 16).reshape(2 * RANK, HALF)
    sent_ranks = swap(ranks, "x_lo")

    cross = (cross_v, cross_u, cross_bias.reshape(FEATS, 1), upstream_t)
    crossed, own, other = first_backward(at_keep, kept_words, ranks, kept_pooled, *cross)
    crossed, grads, cross_grads, other = second_backward(
        at_sent, other_words, sent_ranks, sent_pooled, *cross, other, crossed
    )
    from_other = to_other_core(other)
    own = rest_of_backward(at_sent, own_words, grads, cross_grads, own)

    chip_sum = (own.astype(f32) + from_other.astype(f32)).astype(bf16)
    sums = jnp.sum(exchange(chip_sum, DP_OUTER).astype(f32), axis=0)
    row_grad = exchange(sums[:FEATS].astype(bf16).T.reshape(N_ROW, PART, FEATS), ROW_AXES)
    my_accum = lax.dynamic_slice(accum, (0, part * PART), (TABLES, PART))
    my_accum = jnp.broadcast_to(my_accum[:, :, None], (TABLES, PART, WIDTH)).reshape(TABLES * PART, WIDTH)

    own = exchange(
        adagrad(row_grad, my_rows.reshape(TABLES * PART, WIDTH), my_accum, sums[FEATS:]), DP_OUTER
    )
    new_rows, new_accum, grad_v, grad_u, grad_bias = unpack(
        jnp.stack([core]).astype(jnp.int32), own, to_other_core(own)
    )
    return (crossed.T, new_rows.reshape(TABLES, ROWS, WIDTH), new_accum, grad_v, grad_u, grad_bias)


def solution(mesh):
    inner = Mesh(mesh.devices.reshape(4, 2, 2, 2, 16), ("y", "x_hi", "core", "x_lo", "z"))
    dp = ("y", "x_hi", "core")
    row = ROW_ALL
    return jax.shard_map(
        body,
        mesh=inner,
        in_specs=(
            P(None, row, None),
            P(None, row),
            P(dp, None, None),
            P(row, None),
            P(row, None),
            P(row),
            P(dp, row),
        ),
        out_specs=(
            P(dp, row),
            P(None, row, None),
            P(None, row),
            P(row, None),
            P(row, None),
            P(row),
        ),
        check_vma=False,
    )
```

```python
import functools

import jax
import jax.numpy as jnp
from jax import lax
from jax.experimental import pallas as pl
from jax.experimental.pallas import tpu as pltpu
from jax.sharding import Mesh
from jax.sharding import PartitionSpec as P

bf16 = jnp.bfloat16
f32 = jnp.float32
learn_rate = 0.3
epsilon = 1e-06

SAMPLES, TABLES, BAG, ROWS, WIDTH, FEATS, RANK = 512, 26, 8, 256, 128, 104, 256
N_ROW, N_DP, PART = 32, 16, 16
STEP_ROWS = N_ROW * PART
WORDS = STEP_ROWS // 8
HALF = SAMPLES // 2
GRAD_ROWS = 8
OUT_ROWS = FEATS + GRAD_ROWS
DP_OUTER = ("x_hi", "y")
ROW_AXES = ("z", "x_lo")
ROW_ALL = ("x_lo", "z")
BLOCK_OF = [(i & 1) * 16 + (i >> 1) for i in range(N_ROW)]
CHUNK = TABLES * PART + 16 + 32
UNROLL = 8
VMEM = 16 << 20

NT_DIMS = (((1,), (1,)), ((), ()))
TN_DIMS = (((0,), (0,)), ((), ()))


def part_of(outer, core):
    return (outer & 3) * 4 + (outer >> 2) * 2 + core


def pieces(table):
    found = []
    for block in range(N_ROW):
        low = max(table * WIDTH, block * FEATS)
        high = min((table + 1) * WIDTH, (block + 1) * FEATS)
        if low < high:
            found.append((block, low - block * FEATS, high - block * FEATS))
    return found


def pack_kernel(scalars, rows, mine, packed):
    mine[...] = rows[...]
    for device, block in enumerate(BLOCK_OF):
        first = block * FEATS // WIDTH
        start = block * FEATS - first * WIDTH
        cut = rows[first][:, start:].astype(f32)
        if cut.shape[1] < FEATS:
            cut = jnp.concatenate([cut, rows[first + 1][:, : FEATS - cut.shape[1]].astype(f32)], axis=1)
        packed[device] = cut[:, :FEATS].astype(bf16)


def pack(scalars, rows):
    return pl.pallas_call(
        pack_kernel,
        grid_spec=pltpu.PrefetchScalarGridSpec(
            num_scalar_prefetch=1,
            grid=(1,),
            in_specs=[pl.BlockSpec((TABLES, PART, WIDTH), lambda g, s: (0, s[0], 0))],
            out_specs=[
                pl.BlockSpec((TABLES, PART, WIDTH), lambda g, s: (0, 0, 0)),
                pl.BlockSpec((N_ROW, PART, FEATS), lambda g, s: (0, 0, 0)),
            ],
        ),
        out_shape=[
            jax.ShapeDtypeStruct((TABLES, PART, WIDTH), bf16),
            jax.ShapeDtypeStruct((N_ROW, PART, FEATS), bf16),
        ],
        name="pack_rows",
    )(scalars, rows)


def adagrad_kernel(grads_in, rows, accum, cross_grads, out):
    device_of = {block: device for device, block in enumerate(BLOCK_OF)}
    grads = [
        jnp.concatenate([grads_in[device_of[block]].astype(f32)[:, low:high] for block, low, high in pieces(table)], axis=1)
        for table in range(TABLES)
    ]
    grad = jnp.concatenate(grads, axis=0)
    square = grad * grad
    high = square.astype(bf16)
    rest = (square - high.astype(f32)).astype(bf16)
    ones = jnp.ones((WIDTH, WIDTH), bf16)
    sums = jnp.dot(high, ones, preferred_element_type=f32) + jnp.dot(rest, ones, preferred_element_type=f32)
    total = accum[...] + sums * (1.0 / WIDTH)
    new = (rows[...].astype(f32) - learn_rate * grad * lax.rsqrt(total + epsilon)).astype(bf16)
    lane = lax.broadcasted_iota(jnp.int32, (PART, WIDTH), 1)
    accum_out = jnp.zeros((PART, WIDTH), f32)
    for table in range(TABLES):
        mine = total[table * PART : (table + 1) * PART]
        high = mine.astype(bf16).astype(f32)
        rest = mine - high
        middle = rest.astype(bf16).astype(f32)
        accum_out = jnp.where(lane == table, high, accum_out)
        accum_out = jnp.where(lane == table + 32, middle, accum_out)
        accum_out = jnp.where(lane == table + 64, rest - middle, accum_out)
    terms = accum_out.astype(bf16)
    wide = cross_grads[...]
    wide = jnp.concatenate([wide[:, at : at + WIDTH] for at in range(0, 2 * RANK, WIDTH)], axis=0).astype(bf16)
    for copy in range(8):
        out[copy, : TABLES * PART, :] = new
        out[copy, TABLES * PART : TABLES * PART + PART, :] = terms
        out[copy, TABLES * PART + PART :, :] = wide


def adagrad(grads, rows, accum, cross_grads):
    return pl.pallas_call(
        adagrad_kernel,
        out_shape=jax.ShapeDtypeStruct((8, CHUNK, WIDTH), bf16),
        compiler_params=pltpu.CompilerParams(vmem_limit_bytes=VMEM),
        name="adagrad",
    )(grads, rows, accum, cross_grads)


def unpack_kernel(scalars, own, other, rows_out, accum_out, grad_v, grad_u, grad_bias, accums, cross_grads):
    for outer in range(8):
        for turn, source in enumerate((own, other)):
            part = part_of(outer, turn ^ scalars[0])
            rows_out[:, pl.ds(part, 1)] = source[outer, : TABLES * PART].reshape(TABLES, 1, PART, WIDTH)
            terms = source[outer, TABLES * PART : TABLES * PART + PART].astype(f32)
            total = terms[:, :32] + terms[:, 32:64] + terms[:, 64:96]
            accums[pl.ds(pl.multiple_of(part * PART, PART), PART), :] = jnp.concatenate(
                [total, jnp.zeros((PART, WIDTH - 32), f32)], axis=1
            )
            wide = source[outer, TABLES * PART + PART :].astype(f32)
            at = pl.multiple_of(part * GRAD_ROWS, GRAD_ROWS)
            for i in range(4):
                cross_grads[pl.ds(at, GRAD_ROWS), i * WIDTH : (i + 1) * WIDTH] = wide[i * 8 : (i + 1) * 8]
    accum_out[...] = accums[...].T[:TABLES]
    grad_u[...] = cross_grads[:FEATS, :RANK]
    grad_v[...] = cross_grads[:FEATS, RANK:]
    grad_bias[...] = cross_grads[FEATS, :FEATS]


def unpack(scalars, own, other):
    shapes = [
        ((TABLES, N_DP, PART, WIDTH), bf16),
        ((TABLES, ROWS), f32),
        ((FEATS, RANK), f32),
        ((FEATS, RANK), f32),
        ((FEATS,), f32),
    ]
    return call(
        unpack_kernel,
        "unpack",
        scalars,
        (own, other),
        [jax.ShapeDtypeStruct(shape, kind) for shape, kind in shapes],
        [pltpu.VMEM((ROWS, WIDTH), f32), pltpu.VMEM((N_DP * GRAD_ROWS, 2 * RANK), f32)],
    )


def counts_of(words, scaled=False):
    columns = []
    for lane in range(0, words.shape[1], 128):
        blocks = []
        for group in range(0, WORDS, 8):
            word = words[group : group + 8, lane : lane + 128]
            if scaled:
                digits = [word & jnp.int32(15 << (4 * j)) for j in range(7)]
            else:
                digits = [lax.shift_right_logical(word, jnp.int32(4 * j)) & 15 for j in range(7)]
            digits.append(lax.shift_right_logical(word, jnp.int32(28)))
            blocks.append(jnp.concatenate(digits, axis=0).astype(f32).astype(bf16))
        columns.append(jnp.concatenate(blocks, axis=0))
    return jnp.concatenate(columns, axis=1)


def words_of(place):
    inside = (place >= 0) & (place < STEP_ROWS)
    word = jnp.where(inside, ((place >> 6) << 3) | (place & 7), -1)
    unit = jnp.left_shift(jnp.int32(1), ((place >> 3) & 7) * 4)
    columns = []
    for lane in range(0, place.shape[1], 128):
        slots = lax.broadcasted_iota(jnp.int32, (WORDS, 128), 0)
        total = jnp.zeros((WORDS, 128), jnp.int32)
        for k in range(BAG):
            here = word[k : k + 1, lane : lane + 128] == slots
            total = total + jnp.where(here, unit[k : k + 1, lane : lane + 128], 0)
        columns.append(total)
    return jnp.concatenate(columns, axis=1)


def whole(*shape):
    return pl.BlockSpec(shape, lambda g, s: (0,) * len(shape))


def words_kernel(scalars, *refs):
    ids, kept, sent, places = refs[:4], refs[4], refs[5:7], refs[7]
    step = pl.program_id(0)

    @pl.when(step == 0)
    def _():
        for i in range(4):
            row = ids[i][0]
            part = (row >> 4) & 15
            turn = (part & 1) ^ scalars[2]
            outer = (((part >> 1) & 1) << 2) | (part >> 2)
            device = (((row >> 8) & 15) << 1) | (row >> 12)
            places[i] = turn * 4096 + outer * 512 + device * 16 + (row & 15)

    for table in range(2):
        for turn in range(2):
            first = (turn * 8 + step) * STEP_ROWS
            kept[table, turn, 0] = words_of(places[table] - first)
            sent[turn][table, 0, 0] = words_of(places[2 + table] - first)


def bag_words(scalars, ids):
    return pl.pallas_call(
        words_kernel,
        grid_spec=pltpu.PrefetchScalarGridSpec(
            num_scalar_prefetch=1,
            grid=(8,),
            in_specs=[
                pl.BlockSpec((1, BAG, HALF), lambda g, s: (s[0], 0, s[3])),
                pl.BlockSpec((1, BAG, HALF), lambda g, s: (s[1], 0, s[3])),
                pl.BlockSpec((1, BAG, HALF), lambda g, s: (s[0], 0, 1 - s[3])),
                pl.BlockSpec((1, BAG, HALF), lambda g, s: (s[1], 0, 1 - s[3])),
            ],
            out_specs=[pl.BlockSpec((2, turns, 1, WORDS, HALF), lambda g, s: (0, 0, g, 0, 0)) for turns in (2, 1, 1)],
            scratch_shapes=[pltpu.VMEM((4, BAG, HALF), jnp.int32)],
        ),
        out_shape=[jax.ShapeDtypeStruct((2, turns, 8, WORDS, HALF), jnp.int32) for turns in (2, 1, 1)],
        compiler_params=pltpu.CompilerParams(vmem_limit_bytes=VMEM),
        cost_estimate=pl.CostEstimate(flops=1 << 28, bytes_accessed=5 << 20, transcendentals=0),
        name="bag_words",
    )(scalars, ids, ids, ids, ids)


KERNEL_COST = pl.CostEstimate(flops=1 << 32, bytes_accessed=5 << 20, transcendentals=0)


def call(kernel, name, scalars, operands, out_shape, scratch_shapes=()):
    return pl.pallas_call(
        kernel,
        in_specs=[pl.BlockSpec(memory_space=pltpu.SMEM)] + [pl.BlockSpec(memory_space=pltpu.VMEM)] * len(operands),
        out_shape=out_shape,
        scratch_shapes=list(scratch_shapes),
        compiler_params=pltpu.CompilerParams(vmem_limit_bytes=VMEM),
        cost_estimate=KERNEL_COST,
        name=name,
    )(scalars, *operands)


def half_of(scalars):
    return pl.ds(pl.multiple_of(scalars[0] * HALF, HALF), HALF)


def forward_kernel(turns, last, scalars, words, *refs):
    rows, refs = refs[:turns], refs[turns:]
    if last:
        *before, pooled_out, total = refs
    else:
        before, total = refs[:-1], refs[-1]
    total[...] = before[0][...] if before else jnp.zeros_like(total)

    @pl.loop(0, 8 // UNROLL)
    def _(step):
        for table in range(2):
            added = None
            for i in range(UNROLL):
                for turn, source in enumerate(rows):
                    counts = counts_of(words[table, turn, step * UNROLL + i], scaled=True)
                    term = jnp.dot(source[step * UNROLL + i], counts, preferred_element_type=f32)
                    added = term if added is None else added + term
            total[table] += added

    if last:
        feature = lax.broadcasted_iota(jnp.int32, (FEATS, HALF), 0)
        pooled_out[...] = jnp.where(feature < scalars[1], total[0], total[1]).astype(bf16)


def forward(scalars, words, rows, before=None, last=True):
    operands = [words, *rows] if before is None else [words, *rows, before]
    if last:
        out_shape, scratch = jax.ShapeDtypeStruct((FEATS, HALF), bf16), [pltpu.VMEM((2, FEATS, HALF), f32)]
    else:
        out_shape, scratch = jax.ShapeDtypeStruct((2, FEATS, HALF), f32), []
    return call(functools.partial(forward_kernel, len(rows), last), "bags", scalars, operands, out_shape, scratch)


def ranks_kernel(scalars, pooled_a, pooled_b, v_a, u_a, upstream_a, partner, ranks):
    rank = jnp.zeros((RANK, HALF), f32)
    rank_grad = jnp.zeros((RANK, HALF), f32)
    sides = (
        (pooled_a[...], v_a[...], u_a[...], upstream_a[:, half_of(scalars)]),
        (pooled_b[...], partner[:, :RANK], partner[:, RANK : 2 * RANK], partner[:, 2 * RANK :]),
    )
    for pooled, v, u, upstream in sides:
        gate_grad = (upstream.astype(f32) * pooled.astype(f32)).astype(bf16)
        rank += lax.dot_general(v, pooled, TN_DIMS, preferred_element_type=f32)
        rank_grad += lax.dot_general(u, gate_grad, TN_DIMS, preferred_element_type=f32)
    ranks[:RANK] = rank.astype(bf16)
    ranks[RANK:] = rank_grad.astype(bf16)


def rank_terms(scalars, *operands):
    return call(ranks_kernel, "rank_terms", scalars, operands, jax.ShapeDtypeStruct((2 * RANK, HALF), bf16))


def sum_and_copy_kernel(terms, out):
    total = terms[0].astype(f32)
    for i in range(1, terms.shape[0]):
        total = total + terms[i].astype(f32)
    total = total.astype(bf16)
    for i in range(out.shape[0]):
        out[i] = total


def sum_and_copy(terms):
    return pl.pallas_call(
        sum_and_copy_kernel,
        out_shape=jax.ShapeDtypeStruct(terms.shape, bf16),
        compiler_params=pltpu.CompilerParams(vmem_limit_bytes=VMEM),
        name="sum_and_copy",
    )(terms)


def sum_and_turn_kernel(terms, grads, cross_grads):
    total = terms[0].astype(f32)
    for i in range(1, 8):
        total = total + terms[i].astype(f32)
    grads[...] = total[:FEATS].T.astype(bf16)
    cross_grads[...] = total[FEATS:]


def sum_and_turn(terms):
    return pl.pallas_call(
        sum_and_turn_kernel,
        out_shape=[
            jax.ShapeDtypeStruct((STEP_ROWS, FEATS), bf16),
            jax.ShapeDtypeStruct((GRAD_ROWS, 2 * RANK), f32),
        ],
        compiler_params=pltpu.CompilerParams(vmem_limit_bytes=VMEM),
        name="sum_and_turn",
    )(terms)


def cross_layer(scalars, ranks, pooled_in, v, u, bias, upstream_in, grads, cross_grads):
    rank = ranks[:RANK]
    rank_grad = ranks[RANK:]
    pooled_bf = pooled_in[...]
    pooled = pooled_bf.astype(f32)
    upstream = upstream_in[:, half_of(scalars)].astype(f32)
    gate = jnp.dot(u[...], rank, preferred_element_type=f32) + bias[...]
    crossed = (pooled * gate + pooled).astype(bf16)
    back = jnp.dot(v[...], rank_grad, preferred_element_type=f32)
    grad = (upstream * (gate + 1.0) + back).astype(bf16).astype(f32)
    feature = lax.broadcasted_iota(jnp.int32, (FEATS, HALF), 0)
    grads[0] = jnp.where(feature < scalars[1], grad, 0.0).astype(bf16)
    grads[1] = jnp.where(feature < scalars[1], 0.0, grad).astype(bf16)
    gate_grad = upstream * pooled
    gate_bf = gate_grad.astype(bf16)
    gate_rest = (gate_grad - gate_bf.astype(f32)).astype(bf16)
    cross_grads[...] = jnp.zeros_like(cross_grads)
    cross_grads[:FEATS, :RANK] = lax.dot_general(gate_bf, rank, NT_DIMS, preferred_element_type=f32)
    cross_grads[:FEATS, RANK:] = lax.dot_general(pooled_bf, rank_grad, NT_DIMS, preferred_element_type=f32)
    ones = jnp.ones((16, HALF), bf16)
    bias_sum = lax.dot_general(ones, gate_bf, NT_DIMS, preferred_element_type=f32) + lax.dot_general(
        ones, gate_rest, NT_DIMS, preferred_element_type=f32
    )
    cross_grads[FEATS : FEATS + 8, :FEATS] = bias_sum[:8]
    return crossed


def row_grads(scalars, turns, words, grads, cross_grads, before, outs):
    @pl.loop(0, 8 // UNROLL)
    def _(step):
        for i in range(UNROLL):
            at = step * UNROLL + i
            for n, turn in enumerate(turns):
                part = part_of(at, turn ^ scalars[2])
                result = lax.dot_general(grads[0], counts_of(words[0, n, at]), NT_DIMS, preferred_element_type=f32)
                result += lax.dot_general(grads[1], counts_of(words[1, n, at]), NT_DIMS, preferred_element_type=f32)
                extra = cross_grads[pl.ds(pl.multiple_of(part * GRAD_ROWS, GRAD_ROWS), GRAD_ROWS), :]
                block = jnp.concatenate([result, extra], axis=0)
                if before is not None:
                    block = block + before[at]
                outs[n][at] = block.astype(outs[n].dtype)


def first_kernel(scalars, words, ranks, pooled, v, u, bias, upstream, crossed, own, other, grads, cross_grads):
    crossed[...] = cross_layer(scalars, ranks, pooled, v, u, bias, upstream, grads, cross_grads)
    row_grads(scalars, (0, 1), words, grads, cross_grads, None, (own, other))


def second_kernel(
    scalars, words, ranks, pooled, v, u, bias, upstream, before, first, crossed, grads, cross_grads, other
):
    mine = cross_layer(scalars, ranks, pooled, v, u, bias, upstream, grads, cross_grads)
    crossed[:, half_of(scalars)] = mine
    crossed[:, pl.ds(pl.multiple_of((1 - scalars[0]) * HALF, HALF), HALF)] = first[...]
    row_grads(scalars, (1,), words, grads, cross_grads, before, (other,))


def rest_kernel(scalars, words, grads, cross_grads, before, own):
    row_grads(scalars, (0,), words, grads, cross_grads, before, (own,))


SUMS = (8, OUT_ROWS, STEP_ROWS)
GRADS = (2, FEATS, HALF)
CROSS_GRADS = (N_DP * GRAD_ROWS, 2 * RANK)


def first_backward(scalars, *operands):
    return call(
        first_kernel,
        "cross_and_row_grads",
        scalars,
        operands,
        [jax.ShapeDtypeStruct((FEATS, HALF), bf16), jax.ShapeDtypeStruct(SUMS, f32), jax.ShapeDtypeStruct(SUMS, f32)],
        [pltpu.VMEM(GRADS, bf16), pltpu.VMEM(CROSS_GRADS, f32)],
    )


def second_backward(scalars, *operands):
    return call(
        second_kernel,
        "cross_and_row_grads",
        scalars,
        operands,
        [
            jax.ShapeDtypeStruct((FEATS, SAMPLES), bf16),
            jax.ShapeDtypeStruct(GRADS, bf16),
            jax.ShapeDtypeStruct(CROSS_GRADS, f32),
            jax.ShapeDtypeStruct(SUMS, bf16),
        ],
    )


def rest_of_backward(scalars, *operands):
    return call(rest_kernel, "row_grads", scalars, operands, jax.ShapeDtypeStruct(SUMS, bf16))


def exchange(x, axes):
    return lax.all_to_all(x, axes, 0, 0, tiled=True)


def swap(x, axis):
    return lax.ppermute(x, axis, [(0, 1), (1, 0)])


def to_other_core(x):
    return swap(x, "core")


def body(rows_in, accum, bag_ids, cross_v, cross_u, cross_bias, upstream):
    block = lax.axis_index("x_lo") * 16 + lax.axis_index("z")
    core = lax.axis_index("core")
    part = part_of(lax.axis_index(DP_OUTER), core)
    table_a = (block * FEATS) // WIDTH
    table_b = jnp.minimum(table_a + 1, TABLES - 1)
    n_a = jnp.minimum(FEATS, WIDTH * (table_a + 1) - FEATS * block)

    upstream_t = upstream.T
    sent_upstream = lax.dynamic_slice(upstream_t, (0, (1 - lax.axis_index("x_lo")) * HALF), (FEATS, HALF))
    partner = swap(jnp.concatenate([cross_v, cross_u, sent_upstream], axis=1), "x_lo")

    my_rows, packed = pack(jnp.stack([part]).astype(jnp.int32), rows_in)
    mine = exchange(packed, ROW_AXES).reshape(STEP_ROWS, FEATS).T
    nibble = (jnp.arange(STEP_ROWS) >> 3) & 7
    mine = mine * jnp.where(nibble == 7, 1.0, jnp.exp2(-4.0 * nibble)).astype(bf16)
    mine, partner = lax.optimization_barrier((mine, partner))
    own = exchange(jnp.broadcast_to(mine, (8, FEATS, STEP_ROWS)), DP_OUTER)

    keep = lax.axis_index("x_lo")
    scalars = jnp.stack([table_a, table_b, core, keep]).astype(jnp.int32)
    at_keep = jnp.stack([keep, n_a, core]).astype(jnp.int32)
    at_sent = jnp.stack([1 - keep, n_a, core]).astype(jnp.int32)
    ids = bag_ids.transpose(1, 2, 0)
    words = bag_words(scalars, ids)
    own, kept_words, own_words, other_words = lax.optimization_barrier((own, *words))
    other = to_other_core(own)

    sent_sums = forward(at_sent, own_words, [own], last=False)
    sent_pooled = forward(at_sent, other_words, [other], before=sent_sums)
    partner_pooled = swap(sent_pooled, "x_lo")
    kept_pooled = forward(at_keep, kept_words, [own, other])

    terms = rank_terms(at_keep, kept_pooled, partner_pooled, cross_v, cross_u, upstream_t, partner)
    chunks = sum_and_copy(exchange(terms.reshape(16, 32, HALF), "z"))
    ranks = exchange(chunks, "z").reshape(2 * RANK, HALF)
    sent_ranks = swap(ranks, "x_lo")

    cross = (cross_v, cross_u, cross_bias.reshape(FEATS, 1), upstream_t)
    crossed, own, other = first_backward(at_keep, kept_words, ranks, kept_pooled, *cross)
    crossed, grads, cross_grads, other = second_backward(
        at_sent, other_words, sent_ranks, sent_pooled, *cross, other, crossed
    )
    from_other = to_other_core(other)
    own = rest_of_backward(at_sent, own_words, grads, cross_grads, own)

    chip_sum = (own.astype(f32) + from_other.astype(f32)).astype(bf16)
    row_grad, cross_sums = sum_and_turn(exchange(chip_sum, DP_OUTER))
    row_grad = exchange(row_grad.reshape(N_ROW, PART, FEATS), ROW_AXES)
    my_accum = lax.dynamic_slice(accum, (0, part * PART), (TABLES, PART))
    my_accum = jnp.broadcast_to(my_accum[:, :, None], (TABLES, PART, WIDTH)).reshape(TABLES * PART, WIDTH)

    own = exchange(
        adagrad(row_grad, my_rows.reshape(TABLES * PART, WIDTH), my_accum, cross_sums), DP_OUTER
    )
    new_rows, new_accum, grad_v, grad_u, grad_bias = unpack(
        jnp.stack([core]).astype(jnp.int32), own, to_other_core(own)
    )
    return (crossed.T, new_rows.reshape(TABLES, ROWS, WIDTH), new_accum, grad_v, grad_u, grad_bias)


def solution(mesh):
    inner = Mesh(mesh.devices.reshape(4, 2, 2, 2, 16), ("y", "x_hi", "core", "x_lo", "z"))
    dp = ("y", "x_hi", "core")
    row = ROW_ALL
    return jax.shard_map(
        body,
        mesh=inner,
        in_specs=(
            P(None, row, None),
            P(None, row),
            P(dp, None, None),
            P(row, None),
            P(row, None),
            P(row),
            P(dp, row),
        ),
        out_specs=(
            P(dp, row),
            P(None, row, None),
            P(None, row),
            P(row, None),
            P(row, None),
            P(row),
        ),
        check_vma=False,
    )
```

```python
import functools

import jax
import jax.numpy as jnp
from jax import lax
from jax.experimental import pallas as pl
from jax.experimental.pallas import tpu as pltpu
from jax.sharding import Mesh
from jax.sharding import PartitionSpec as P

bf16 = jnp.bfloat16
f32 = jnp.float32
learn_rate = 0.3
epsilon = 1e-06

SAMPLES, TABLES, BAG, ROWS, WIDTH, FEATS, RANK = 512, 26, 8, 256, 128, 104, 256
N_ROW, N_DP, PART = 32, 16, 16
STEP_ROWS = N_ROW * PART
WORDS = STEP_ROWS // 8
HALF = SAMPLES // 2
GRAD_ROWS = 8
OUT_ROWS = FEATS + GRAD_ROWS
DP_OUTER = ("x_hi", "y")
ROW_AXES = ("z", "x_lo")
ROW_ALL = ("x_lo", "z")
BLOCK_OF = [(i & 1) * 16 + (i >> 1) for i in range(N_ROW)]
CHUNK = (TABLES + 3, PART, WIDTH)
UNROLL = 8
VMEM = 16 << 20

NT_DIMS = (((1,), (1,)), ((), ()))
TN_DIMS = (((0,), (0,)), ((), ()))


def part_of(outer, core):
    return (outer & 3) * 4 + (outer >> 2) * 2 + core


def pieces(table):
    found = []
    for block in range(N_ROW):
        low = max(table * WIDTH, block * FEATS)
        high = min((table + 1) * WIDTH, (block + 1) * FEATS)
        if low < high:
            found.append((block, low - block * FEATS, high - block * FEATS))
    return found


def pack_kernel(scalars, rows, mine, packed):
    mine[...] = rows[...]
    for device, block in enumerate(BLOCK_OF):
        first = block * FEATS // WIDTH
        start = block * FEATS - first * WIDTH
        cut = rows[first][:, start:].astype(f32)
        if cut.shape[1] < FEATS:
            cut = jnp.concatenate([cut, rows[first + 1][:, : FEATS - cut.shape[1]].astype(f32)], axis=1)
        packed[device] = cut[:, :FEATS].astype(bf16)


def pack(scalars, rows):
    return pl.pallas_call(
        pack_kernel,
        grid_spec=pltpu.PrefetchScalarGridSpec(
            num_scalar_prefetch=1,
            grid=(1,),
            in_specs=[pl.BlockSpec((TABLES, PART, WIDTH), lambda g, s: (0, s[0], 0))],
            out_specs=[
                pl.BlockSpec((TABLES, PART, WIDTH), lambda g, s: (0, 0, 0)),
                pl.BlockSpec((N_ROW, PART, FEATS), lambda g, s: (0, 0, 0)),
            ],
        ),
        out_shape=[
            jax.ShapeDtypeStruct((TABLES, PART, WIDTH), bf16),
            jax.ShapeDtypeStruct((N_ROW, PART, FEATS), bf16),
        ],
        name="pack_rows",
    )(scalars, rows)


def adagrad_kernel(grads_in, rows, accum, cross_grads, out):
    device_of = {block: device for device, block in enumerate(BLOCK_OF)}
    grads = [
        jnp.concatenate([grads_in[device_of[block]].astype(f32)[:, low:high] for block, low, high in pieces(table)], axis=1)
        for table in range(TABLES)
    ]
    grad = jnp.concatenate(grads, axis=0)
    square = grad * grad
    high = square.astype(bf16)
    rest = (square - high.astype(f32)).astype(bf16)
    ones = jnp.ones((WIDTH, WIDTH), bf16)
    sums = jnp.dot(high, ones, preferred_element_type=f32) + jnp.dot(rest, ones, preferred_element_type=f32)
    total = accum[...] + sums * (1.0 / WIDTH)
    new = (rows[...].astype(f32) - learn_rate * grad * lax.rsqrt(total + epsilon)).astype(bf16)
    lane = lax.broadcasted_iota(jnp.int32, (PART, WIDTH), 1)
    accum_out = jnp.zeros((PART, WIDTH), f32)
    for table in range(TABLES):
        mine = total[table * PART : (table + 1) * PART]
        high = mine.astype(bf16).astype(f32)
        rest = mine - high
        middle = rest.astype(bf16).astype(f32)
        accum_out = jnp.where(lane == table, high, accum_out)
        accum_out = jnp.where(lane == table + 32, middle, accum_out)
        accum_out = jnp.where(lane == table + 64, rest - middle, accum_out)
    terms = accum_out.astype(bf16)
    wide = cross_grads[...]
    wide = jnp.concatenate([wide[:, at : at + WIDTH] for at in range(0, 2 * RANK, WIDTH)], axis=0).astype(bf16)
    for copy in range(8):
        out[copy, :TABLES] = new.reshape(TABLES, PART, WIDTH)
        out[copy, TABLES] = terms
        out[copy, TABLES + 1 :] = wide.reshape(2, PART, WIDTH)


def adagrad(grads, rows, accum, cross_grads):
    return pl.pallas_call(
        adagrad_kernel,
        out_shape=jax.ShapeDtypeStruct((8, *CHUNK), bf16),
        compiler_params=pltpu.CompilerParams(vmem_limit_bytes=VMEM),
        name="adagrad",
    )(grads, rows, accum, cross_grads)


def start_rows(source, rows_out, turn, scalars, arrived):
    copies = []
    for outer in range(8):
        part = part_of(outer, turn ^ scalars[0])
        copies.append(
            pltpu.make_async_copy(source.at[outer, pl.ds(0, TABLES)], rows_out.at[:, part], arrived.at[outer])
        )
        copies[-1].start()
    return copies


def place_rest(source, turn, scalars, accums, cross_grads):
    for outer in range(8):
        part = part_of(outer, turn ^ scalars[0])
        terms = source[outer, TABLES].astype(f32)
        total = terms[:, :32] + terms[:, 32:64] + terms[:, 64:96]
        accums[pl.ds(pl.multiple_of(part * PART, PART), PART), :] = jnp.concatenate(
            [total, jnp.zeros((PART, WIDTH - 32), f32)], axis=1
        )
        wide = source[outer, TABLES + 1 :].astype(f32).reshape(2 * PART, WIDTH)
        at = pl.multiple_of(part * GRAD_ROWS, GRAD_ROWS)
        for i in range(4):
            cross_grads[pl.ds(at, GRAD_ROWS), i * WIDTH : (i + 1) * WIDTH] = wide[i * 8 : (i + 1) * 8]


def own_rows_kernel(scalars, own, rows_out, accums, cross_grads, arrived):
    copies = start_rows(own, rows_out, 0, scalars, arrived)
    accums[...] = jnp.zeros_like(accums)
    cross_grads[...] = jnp.zeros_like(cross_grads)
    place_rest(own, 0, scalars, accums, cross_grads)
    for copy in copies:
        copy.wait()


def unpack_kernel(
    scalars, other, own_accums, own_cross, _, rows_out, accum_out, grad_v, grad_u, grad_bias, accums, cross_grads, arrived
):
    copies = start_rows(other, rows_out, 1, scalars, arrived)
    accums[...] = own_accums[...]
    cross_grads[...] = own_cross[...]
    place_rest(other, 1, scalars, accums, cross_grads)
    accum_out[...] = accums[...].T[:TABLES]
    grad_u[...] = cross_grads[:FEATS, :RANK]
    grad_v[...] = cross_grads[:FEATS, RANK:]
    grad_bias[...] = cross_grads[FEATS, :FEATS]
    for copy in copies:
        copy.wait()


NEW_ROWS = jax.ShapeDtypeStruct((TABLES, N_DP, PART, WIDTH), bf16)


def own_rows(scalars, own):
    return pl.pallas_call(
        own_rows_kernel,
        in_specs=[pl.BlockSpec(memory_space=pltpu.SMEM), pl.BlockSpec(memory_space=pltpu.VMEM)],
        out_specs=[pl.BlockSpec(memory_space=pl.ANY)] + [pl.BlockSpec(memory_space=pltpu.VMEM)] * 2,
        out_shape=[
            NEW_ROWS,
            jax.ShapeDtypeStruct((ROWS, WIDTH), f32),
            jax.ShapeDtypeStruct((N_DP * GRAD_ROWS, 2 * RANK), f32),
        ],
        scratch_shapes=[pltpu.SemaphoreType.DMA((8,))],
        compiler_params=pltpu.CompilerParams(vmem_limit_bytes=VMEM),
        cost_estimate=pl.CostEstimate(flops=1 << 28, bytes_accessed=2 << 20, transcendentals=0),
        name="own_rows",
    )(scalars, own)


def unpack(scalars, other, rows, accums, cross_grads):
    vmem = pl.BlockSpec(memory_space=pltpu.VMEM)
    any_space = pl.BlockSpec(memory_space=pl.ANY)
    shapes = [(TABLES, ROWS), (FEATS, RANK), (FEATS, RANK), (FEATS,)]
    return pl.pallas_call(
        unpack_kernel,
        in_specs=[pl.BlockSpec(memory_space=pltpu.SMEM), vmem, vmem, vmem, any_space],
        out_specs=[any_space] + [vmem] * len(shapes),
        out_shape=[NEW_ROWS] + [jax.ShapeDtypeStruct(shape, f32) for shape in shapes],
        input_output_aliases={4: 0},
        scratch_shapes=[
            pltpu.VMEM((ROWS, WIDTH), f32),
            pltpu.VMEM((N_DP * GRAD_ROWS, 2 * RANK), f32),
            pltpu.SemaphoreType.DMA((8,)),
        ],
        compiler_params=pltpu.CompilerParams(vmem_limit_bytes=VMEM),
        name="unpack",
    )(scalars, other, accums, cross_grads, rows)


def counts_of(words, scaled=False):
    columns = []
    for lane in range(0, words.shape[1], 128):
        blocks = []
        for group in range(0, WORDS, 8):
            word = words[group : group + 8, lane : lane + 128]
            if scaled:
                digits = [word & jnp.int32(15 << (4 * j)) for j in range(7)]
            else:
                digits = [lax.shift_right_logical(word, jnp.int32(4 * j)) & 15 for j in range(7)]
            digits.append(lax.shift_right_logical(word, jnp.int32(28)))
            blocks.append(jnp.concatenate(digits, axis=0).astype(f32).astype(bf16))
        columns.append(jnp.concatenate(blocks, axis=0))
    return jnp.concatenate(columns, axis=1)


def words_of(place):
    inside = (place >= 0) & (place < STEP_ROWS)
    word = jnp.where(inside, ((place >> 6) << 3) | (place & 7), -1)
    unit = jnp.left_shift(jnp.int32(1), ((place >> 3) & 7) * 4)
    columns = []
    for lane in range(0, place.shape[1], 128):
        slots = lax.broadcasted_iota(jnp.int32, (WORDS, 128), 0)
        total = jnp.zeros((WORDS, 128), jnp.int32)
        for k in range(BAG):
            here = word[k : k + 1, lane : lane + 128] == slots
            total = total + jnp.where(here, unit[k : k + 1, lane : lane + 128], 0)
        columns.append(total)
    return jnp.concatenate(columns, axis=1)


def whole(*shape):
    return pl.BlockSpec(shape, lambda g, s: (0,) * len(shape))


def words_kernel(scalars, *refs):
    ids, kept, sent, places = refs[:4], refs[4], refs[5:7], refs[7]
    step = pl.program_id(0)

    @pl.when(step == 0)
    def _():
        for i in range(4):
            row = ids[i][0]
            part = (row >> 4) & 15
            turn = (part & 1) ^ scalars[2]
            outer = (((part >> 1) & 1) << 2) | (part >> 2)
            device = (((row >> 8) & 15) << 1) | (row >> 12)
            places[i] = turn * 4096 + outer * 512 + device * 16 + (row & 15)

    for table in range(2):
        for turn in range(2):
            first = (turn * 8 + step) * STEP_ROWS
            kept[table, turn, 0] = words_of(places[table] - first)
            sent[turn][table, 0, 0] = words_of(places[2 + table] - first)


def bag_words(scalars, ids):
    return pl.pallas_call(
        words_kernel,
        grid_spec=pltpu.PrefetchScalarGridSpec(
            num_scalar_prefetch=1,
            grid=(8,),
            in_specs=[
                pl.BlockSpec((1, BAG, HALF), lambda g, s: (s[0], 0, s[3])),
                pl.BlockSpec((1, BAG, HALF), lambda g, s: (s[1], 0, s[3])),
                pl.BlockSpec((1, BAG, HALF), lambda g, s: (s[0], 0, 1 - s[3])),
                pl.BlockSpec((1, BAG, HALF), lambda g, s: (s[1], 0, 1 - s[3])),
            ],
            out_specs=[pl.BlockSpec((2, turns, 1, WORDS, HALF), lambda g, s: (0, 0, g, 0, 0)) for turns in (2, 1, 1)],
            scratch_shapes=[pltpu.VMEM((4, BAG, HALF), jnp.int32)],
        ),
        out_shape=[jax.ShapeDtypeStruct((2, turns, 8, WORDS, HALF), jnp.int32) for turns in (2, 1, 1)],
        compiler_params=pltpu.CompilerParams(vmem_limit_bytes=VMEM),
        cost_estimate=pl.CostEstimate(flops=1 << 28, bytes_accessed=5 << 20, transcendentals=0),
        name="bag_words",
    )(scalars, ids, ids, ids, ids)


KERNEL_COST = pl.CostEstimate(flops=1 << 32, bytes_accessed=5 << 20, transcendentals=0)


def call(kernel, name, scalars, operands, out_shape, scratch_shapes=()):
    return pl.pallas_call(
        kernel,
        in_specs=[pl.BlockSpec(memory_space=pltpu.SMEM)] + [pl.BlockSpec(memory_space=pltpu.VMEM)] * len(operands),
        out_shape=out_shape,
        scratch_shapes=list(scratch_shapes),
        compiler_params=pltpu.CompilerParams(vmem_limit_bytes=VMEM),
        cost_estimate=KERNEL_COST,
        name=name,
    )(scalars, *operands)


def half_of(scalars):
    return pl.ds(pl.multiple_of(scalars[0] * HALF, HALF), HALF)


def forward_kernel(turns, last, scalars, words, *refs):
    rows, refs = refs[:turns], refs[turns:]
    if last:
        *before, pooled_out, total = refs
    else:
        before, total = refs[:-1], refs[-1]
    total[...] = before[0][...] if before else jnp.zeros_like(total)

    @pl.loop(0, 8 // UNROLL)
    def _(step):
        for table in range(2):
            added = None
            for i in range(UNROLL):
                for turn, source in enumerate(rows):
                    counts = counts_of(words[table, turn, step * UNROLL + i], scaled=True)
                    term = jnp.dot(source[step * UNROLL + i], counts, preferred_element_type=f32)
                    added = term if added is None else added + term
            total[table] += added

    if last:
        feature = lax.broadcasted_iota(jnp.int32, (FEATS, HALF), 0)
        pooled_out[...] = jnp.where(feature < scalars[1], total[0], total[1]).astype(bf16)


def forward(scalars, words, rows, before=None, last=True):
    operands = [words, *rows] if before is None else [words, *rows, before]
    if last:
        out_shape, scratch = jax.ShapeDtypeStruct((FEATS, HALF), bf16), [pltpu.VMEM((2, FEATS, HALF), f32)]
    else:
        out_shape, scratch = jax.ShapeDtypeStruct((2, FEATS, HALF), f32), []
    return call(functools.partial(forward_kernel, len(rows), last), "bags", scalars, operands, out_shape, scratch)


def ranks_kernel(scalars, pooled_a, pooled_b, v_a, u_a, upstream_a, partner, ranks):
    rank = jnp.zeros((RANK, HALF), f32)
    rank_grad = jnp.zeros((RANK, HALF), f32)
    sides = (
        (pooled_a[...], v_a[...], u_a[...], upstream_a[:, half_of(scalars)]),
        (pooled_b[...], partner[:, :RANK], partner[:, RANK : 2 * RANK], partner[:, 2 * RANK :]),
    )
    for pooled, v, u, upstream in sides:
        gate_grad = (upstream.astype(f32) * pooled.astype(f32)).astype(bf16)
        rank += lax.dot_general(v, pooled, TN_DIMS, preferred_element_type=f32)
        rank_grad += lax.dot_general(u, gate_grad, TN_DIMS, preferred_element_type=f32)
    ranks[:RANK] = rank.astype(bf16)
    ranks[RANK:] = rank_grad.astype(bf16)


def rank_terms(scalars, *operands):
    return call(ranks_kernel, "rank_terms", scalars, operands, jax.ShapeDtypeStruct((2 * RANK, HALF), bf16))


def sum_and_copy_kernel(terms, out):
    total = terms[0].astype(f32)
    for i in range(1, terms.shape[0]):
        total = total + terms[i].astype(f32)
    total = total.astype(bf16)
    for i in range(out.shape[0]):
        out[i] = total


def sum_and_copy(terms):
    return pl.pallas_call(
        sum_and_copy_kernel,
        out_shape=jax.ShapeDtypeStruct(terms.shape, bf16),
        compiler_params=pltpu.CompilerParams(vmem_limit_bytes=VMEM),
        name="sum_and_copy",
    )(terms)


def sum_and_turn_kernel(terms, grads, cross_grads):
    total = terms[0].astype(f32)
    for i in range(1, 8):
        total = total + terms[i].astype(f32)
    grads[...] = total[:FEATS].T.astype(bf16)
    cross_grads[...] = total[FEATS:]


def sum_and_turn(terms):
    return pl.pallas_call(
        sum_and_turn_kernel,
        out_shape=[
            jax.ShapeDtypeStruct((STEP_ROWS, FEATS), bf16),
            jax.ShapeDtypeStruct((GRAD_ROWS, 2 * RANK), f32),
        ],
        compiler_params=pltpu.CompilerParams(vmem_limit_bytes=VMEM),
        name="sum_and_turn",
    )(terms)


def cross_layer(scalars, ranks, pooled_in, v, u, bias, upstream_in, grads, cross_grads):
    rank = ranks[:RANK]
    rank_grad = ranks[RANK:]
    pooled_bf = pooled_in[...]
    pooled = pooled_bf.astype(f32)
    upstream = upstream_in[:, half_of(scalars)].astype(f32)
    gate = jnp.dot(u[...], rank, preferred_element_type=f32) + bias[...]
    crossed = (pooled * gate + pooled).astype(bf16)
    back = jnp.dot(v[...], rank_grad, preferred_element_type=f32)
    grad = (upstream * (gate + 1.0) + back).astype(bf16).astype(f32)
    feature = lax.broadcasted_iota(jnp.int32, (FEATS, HALF), 0)
    grads[0] = jnp.where(feature < scalars[1], grad, 0.0).astype(bf16)
    grads[1] = jnp.where(feature < scalars[1], 0.0, grad).astype(bf16)
    gate_grad = upstream * pooled
    gate_bf = gate_grad.astype(bf16)
    gate_rest = (gate_grad - gate_bf.astype(f32)).astype(bf16)
    cross_grads[...] = jnp.zeros_like(cross_grads)
    cross_grads[:FEATS, :RANK] = lax.dot_general(gate_bf, rank, NT_DIMS, preferred_element_type=f32)
    cross_grads[:FEATS, RANK:] = lax.dot_general(pooled_bf, rank_grad, NT_DIMS, preferred_element_type=f32)
    ones = jnp.ones((16, HALF), bf16)
    bias_sum = lax.dot_general(ones, gate_bf, NT_DIMS, preferred_element_type=f32) + lax.dot_general(
        ones, gate_rest, NT_DIMS, preferred_element_type=f32
    )
    cross_grads[FEATS : FEATS + 8, :FEATS] = bias_sum[:8]
    return crossed


def row_grads(scalars, turns, words, grads, cross_grads, before, outs):
    @pl.loop(0, 8 // UNROLL)
    def _(step):
        for i in range(UNROLL):
            at = step * UNROLL + i
            for n, turn in enumerate(turns):
                part = part_of(at, turn ^ scalars[2])
                result = lax.dot_general(grads[0], counts_of(words[0, n, at]), NT_DIMS, preferred_element_type=f32)
                result += lax.dot_general(grads[1], counts_of(words[1, n, at]), NT_DIMS, preferred_element_type=f32)
                extra = cross_grads[pl.ds(pl.multiple_of(part * GRAD_ROWS, GRAD_ROWS), GRAD_ROWS), :]
                block = jnp.concatenate([result, extra], axis=0)
                if before is not None:
                    block = block + before[at]
                outs[n][at] = block.astype(outs[n].dtype)


def first_kernel(scalars, words, ranks, pooled, v, u, bias, upstream, crossed, own, other, grads, cross_grads):
    crossed[...] = cross_layer(scalars, ranks, pooled, v, u, bias, upstream, grads, cross_grads)
    row_grads(scalars, (0, 1), words, grads, cross_grads, None, (own, other))


def second_kernel(
    scalars, words, ranks, pooled, v, u, bias, upstream, before, first, crossed, grads, cross_grads, other
):
    mine = cross_layer(scalars, ranks, pooled, v, u, bias, upstream, grads, cross_grads)
    crossed[:, half_of(scalars)] = mine
    crossed[:, pl.ds(pl.multiple_of((1 - scalars[0]) * HALF, HALF), HALF)] = first[...]
    row_grads(scalars, (1,), words, grads, cross_grads, before, (other,))


def rest_kernel(scalars, words, grads, cross_grads, before, own):
    row_grads(scalars, (0,), words, grads, cross_grads, before, (own,))


SUMS = (8, OUT_ROWS, STEP_ROWS)
GRADS = (2, FEATS, HALF)
CROSS_GRADS = (N_DP * GRAD_ROWS, 2 * RANK)


def first_backward(scalars, *operands):
    return call(
        first_kernel,
        "cross_and_row_grads",
        scalars,
        operands,
        [jax.ShapeDtypeStruct((FEATS, HALF), bf16), jax.ShapeDtypeStruct(SUMS, f32), jax.ShapeDtypeStruct(SUMS, f32)],
        [pltpu.VMEM(GRADS, bf16), pltpu.VMEM(CROSS_GRADS, f32)],
    )


def second_backward(scalars, *operands):
    return call(
        second_kernel,
        "cross_and_row_grads",
        scalars,
        operands,
        [
            jax.ShapeDtypeStruct((FEATS, SAMPLES), bf16),
            jax.ShapeDtypeStruct(GRADS, bf16),
            jax.ShapeDtypeStruct(CROSS_GRADS, f32),
            jax.ShapeDtypeStruct(SUMS, bf16),
        ],
    )


def rest_of_backward(scalars, *operands):
    return call(rest_kernel, "row_grads", scalars, operands, jax.ShapeDtypeStruct(SUMS, bf16))


def exchange(x, axes):
    return lax.all_to_all(x, axes, 0, 0, tiled=True)


def swap(x, axis):
    return lax.ppermute(x, axis, [(0, 1), (1, 0)])


def to_other_core(x):
    return swap(x, "core")


def body(rows_in, accum, bag_ids, cross_v, cross_u, cross_bias, upstream):
    block = lax.axis_index("x_lo") * 16 + lax.axis_index("z")
    core = lax.axis_index("core")
    part = part_of(lax.axis_index(DP_OUTER), core)
    table_a = (block * FEATS) // WIDTH
    table_b = jnp.minimum(table_a + 1, TABLES - 1)
    n_a = jnp.minimum(FEATS, WIDTH * (table_a + 1) - FEATS * block)

    upstream_t = upstream.T
    sent_upstream = lax.dynamic_slice(upstream_t, (0, (1 - lax.axis_index("x_lo")) * HALF), (FEATS, HALF))
    partner = swap(jnp.concatenate([cross_v, cross_u, sent_upstream], axis=1), "x_lo")

    my_rows, packed = pack(jnp.stack([part]).astype(jnp.int32), rows_in)
    mine = exchange(packed, ROW_AXES).reshape(STEP_ROWS, FEATS).T
    nibble = (jnp.arange(STEP_ROWS) >> 3) & 7
    mine = mine * jnp.where(nibble == 7, 1.0, jnp.exp2(-4.0 * nibble)).astype(bf16)
    mine, partner = lax.optimization_barrier((mine, partner))
    own = exchange(jnp.broadcast_to(mine, (8, FEATS, STEP_ROWS)), DP_OUTER)

    keep = lax.axis_index("x_lo")
    scalars = jnp.stack([table_a, table_b, core, keep]).astype(jnp.int32)
    at_keep = jnp.stack([keep, n_a, core]).astype(jnp.int32)
    at_sent = jnp.stack([1 - keep, n_a, core]).astype(jnp.int32)
    ids = bag_ids.transpose(1, 2, 0)
    words = bag_words(scalars, ids)
    own, kept_words, own_words, other_words = lax.optimization_barrier((own, *words))
    other = to_other_core(own)

    sent_sums = forward(at_sent, own_words, [own], last=False)
    sent_pooled = forward(at_sent, other_words, [other], before=sent_sums)
    partner_pooled = swap(sent_pooled, "x_lo")
    kept_pooled = forward(at_keep, kept_words, [own, other])

    terms = rank_terms(at_keep, kept_pooled, partner_pooled, cross_v, cross_u, upstream_t, partner)
    chunks = sum_and_copy(exchange(terms.reshape(16, 32, HALF), "z"))
    ranks = exchange(chunks, "z").reshape(2 * RANK, HALF)
    sent_ranks = swap(ranks, "x_lo")

    cross = (cross_v, cross_u, cross_bias.reshape(FEATS, 1), upstream_t)
    crossed, own, other = first_backward(at_keep, kept_words, ranks, kept_pooled, *cross)
    crossed, grads, cross_grads, other = second_backward(
        at_sent, other_words, sent_ranks, sent_pooled, *cross, other, crossed
    )
    from_other = to_other_core(other)
    own = rest_of_backward(at_sent, own_words, grads, cross_grads, own)

    chip_sum = (own.astype(f32) + from_other.astype(f32)).astype(bf16)
    row_grad, cross_sums = sum_and_turn(exchange(chip_sum, DP_OUTER))
    row_grad = exchange(row_grad.reshape(N_ROW, PART, FEATS), ROW_AXES)
    my_accum = lax.dynamic_slice(accum, (0, part * PART), (TABLES, PART))
    my_accum = jnp.broadcast_to(my_accum[:, :, None], (TABLES, PART, WIDTH)).reshape(TABLES * PART, WIDTH)

    own = exchange(
        adagrad(row_grad, my_rows.reshape(TABLES * PART, WIDTH), my_accum, cross_sums), DP_OUTER
    )
    scalars = jnp.stack([core]).astype(jnp.int32)
    new_rows, new_accum, grad_v, grad_u, grad_bias = unpack(
        scalars, to_other_core(own), *own_rows(scalars, own)
    )
    return (crossed.T, new_rows.reshape(TABLES, ROWS, WIDTH), new_accum, grad_v, grad_u, grad_bias)


def solution(mesh):
    inner = Mesh(mesh.devices.reshape(4, 2, 2, 2, 16), ("y", "x_hi", "core", "x_lo", "z"))
    dp = ("y", "x_hi", "core")
    row = ROW_ALL
    return jax.shard_map(
        body,
        mesh=inner,
        in_specs=(
            P(None, row, None),
            P(None, row),
            P(dp, None, None),
            P(row, None),
            P(row, None),
            P(row),
            P(dp, row),
        ),
        out_specs=(
            P(dp, row),
            P(None, row, None),
            P(None, row),
            P(row, None),
            P(row, None),
            P(row),
        ),
        check_vma=False,
    )
```
